256 devices in a mesh: section: 8 (over y, x_lo), dp: 16 (over z, core), rep: 2 (over x_hi).
Axes of the slice: x: 4 (x_hi: 2, x_lo: 2; x = x_hi * 2 + x_lo), y: 4, z: 8, core: 2. Of those that a mesh axis runs over, the one named last changes fastest.
Arguments:
- enc_weight: bfloat16 [8, 1280, 1280], P('section'), may hold values from -0.15625 to 0.15625
- dec_weight: bfloat16 [8, 1280, 1280], P('section'), may hold values from -0.25 to 0.25
- modulation: bfloat16 [8, 2, 256, 1280], P('section'), may hold values from -0.1796875 to 0.1796875
- enc_inputs: bfloat16 [8, 2, 32, 96, 1280], P('section', None, ('dp', 'rep')), may hold values from -6 to 6
- dec_inputs: bfloat16 [8, 2, 32, 96, 1280], P('section', None, ('dp', 'rep')), may hold values from -6 to 6
- cotangent: bfloat16 [2, 32, 96, 1280], P(None, ('dp', 'rep')), may hold values from -6 to 6
- timesteps: int32 [2, 32, 4], P(None, ('dp', 'rep')), may hold values from 0 to 999
Outputs:
- input_grads: bfloat16 [8, 2, 32, 96, 1280], P('section', None, ('dp', 'rep'))
- grams: float32 [8, 2, 1280, 1280], P('section', None, ('dp', 'rep'))
The draws below stay inside these ranges and needn't reach their ends.
All inputs are finite; a program needn't handle non-finite values.
Results may differ from the reference program's by a relative error of at most 0.023.
Values may be sent and summed in bfloat16 or wider, within the bound.
A program may use at most 64 MiB of HBM per device.

```python
import jax
import jax.numpy as jnp
from jax import lax

C = 1280
EMB = 256
FRAMES = 4
SPATIAL = 24
MB = 2
TOKS = 96
CLIPS = 32
N_SECTION = 8


def touch_ends(values, rng, low, top_value):
    shape = values.shape
    spot = [jax.random.randint(jax.random.fold_in(rng, axis), (), 0, shape[axis]) for axis in range(len(shape))]
    values = values.at[tuple(spot)].set(low)
    longest = shape.index(max(shape))
    spot[longest] = (spot[longest] + 1) % shape[longest]
    return values.at[tuple(spot)].set(top_value)


def shard_levels(own_key, shape, split, least, top_value):
    def one(position, shards_of):
        draws = jax.random.uniform(jax.random.fold_in(jax.random.fold_in(own_key, 6), position), (shards_of,), jnp.float32, least / len(split), top_value / len(split))
        return jnp.repeat(jnp.exp(draws), shape[position] // shards_of).reshape((-1,) + (1,) * (len(shape) - position - 1))

    loudness = one(*split[0])
    for cut in split[1:]:
        loudness = loudness * one(*cut)
    return loudness


def scatter_about(own_key, extent, scale, limit, shards=(), held_as=jnp.bfloat16):
    array = scale * jax.random.normal(own_key, extent, jnp.float32)
    if shards:
        array = array * shard_levels(own_key, extent, shards, -0.22, 0.18)
    return jnp.clip(array, -limit, limit).astype(held_as)


def setup_inputs(seed: int = 0) -> dict:
    streams_of = jax.random.split(jax.random.key(seed), 8)
    return {
        "enc_weight": scatter_about(streams_of[0], (N_SECTION, C, C), C ** -0.5, 0.15625, ((0, 8),)),
        "dec_weight": scatter_about(streams_of[1], (N_SECTION, C, C), (C // 2) ** -0.5, 0.25, ((0, 8),)),
        "modulation": scatter_about(streams_of[2], (N_SECTION, 2, EMB, C), 0.03, 0.1796875, ((0, 8),)),
        "enc_inputs": scatter_about(streams_of[3], (N_SECTION, MB, CLIPS, TOKS, C), 1.0, 6.0, ((0, 8), (2, 32))),
        "dec_inputs": scatter_about(streams_of[4], (N_SECTION, MB, CLIPS, TOKS, C), 1.0, 6.0, ((0, 8), (2, 32))),
        "cotangent": scatter_about(streams_of[5], (MB, CLIPS, TOKS, C), 1.0, 6.0, ((1, 32),)),
        "timesteps": touch_ends(jax.random.randint(streams_of[6], (MB, CLIPS, FRAMES), 0, 1000), jax.random.fold_in(streams_of[6], 1), 0, 999).astype(jnp.int32),
    }


def frame_gain(steps_frames, table):
    half = table.shape[0] // 2
    freqs = jnp.exp(-jnp.log(10000.0) * jnp.arange(half).astype(jnp.float32) / half)
    angles = steps_frames.astype(jnp.float32)[..., None] * freqs
    embedded = jnp.concatenate([jnp.sin(angles), jnp.cos(angles)], axis=-1)
    return 1.0 + jnp.einsum("...e,ed->...d", embedded, table.astype(jnp.float32), precision=lax.Precision.HIGHEST)


def level_back(weight, inputs, row_gain, incoming):
    pre = jnp.dot(inputs, weight, preferred_element_type=jnp.float32) * row_gain
    sigma = jax.nn.sigmoid(pre)
    slope = sigma * (1.0 + pre * (1.0 - sigma))
    pre_grad = (incoming.astype(jnp.float32) * slope * row_gain).astype(jnp.bfloat16)
    back_grad = jnp.dot(pre_grad, weight.T, preferred_element_type=jnp.float32).astype(jnp.bfloat16)
    return back_grad, pre_grad


def gram_total(inputs, grads):
    stacked_in = jnp.transpose(inputs, (1, 0, 2, 3)).reshape(CLIPS, MB * TOKS, C)
    stacked_grad = jnp.transpose(jnp.stack(grads).reshape(MB, CLIPS, TOKS, C), (1, 0, 2, 3)).reshape(CLIPS, MB * TOKS, C)

    def accumulate(total, pair):
        weight_grad = lax.dot_general(pair[0], pair[1], (((0,), (0,)), ((), ())), preferred_element_type=jnp.float32).astype(jnp.bfloat16)
        return total + weight_grad.astype(jnp.float32), None

    total, unused = lax.scan(accumulate, jnp.zeros((C, C), jnp.float32), (stacked_in, stacked_grad))
    summed = total.astype(jnp.bfloat16)
    gram = lax.dot_general(summed, summed, (((0,), (0,)), ((), ())), preferred_element_type=jnp.float32)
    return gram / (C * MB * TOKS * CLIPS)


def reference(enc_weight, dec_weight, modulation, enc_inputs, dec_inputs, cotangent, timesteps):
    rows_all = CLIPS * TOKS

    def gains(level, side, batch_idx):
        per_frame = frame_gain(timesteps[batch_idx], modulation[level, side])
        return jnp.repeat(per_frame, SPATIAL, axis=1).reshape(rows_all, C)

    dec_grads = [[None] * MB for level in range(N_SECTION)]
    enc_grads = [[None] * MB for level in range(N_SECTION)]
    outputs = [[None] * MB for level in range(N_SECTION)]
    for batch_idx in range(MB):
        incoming = cotangent[batch_idx].reshape(rows_all, C)
        skips = []
        for level in range(N_SECTION):
            back_grad, pre_grad = level_back(dec_weight[level], dec_inputs[level, batch_idx].reshape(rows_all, C), gains(level, 1, batch_idx), incoming)
            skips.append(back_grad)
            dec_grads[level][batch_idx] = pre_grad
            incoming = back_grad
        from_above = jnp.zeros((rows_all, C), jnp.bfloat16)
        for level in range(N_SECTION - 1, -1, -1):
            combined = (skips[level].astype(jnp.float32) + from_above.astype(jnp.float32)).astype(jnp.bfloat16)
            back_grad, pre_grad = level_back(enc_weight[level], enc_inputs[level, batch_idx].reshape(rows_all, C), gains(level, 0, batch_idx), combined)
            outputs[level][batch_idx] = back_grad.reshape(CLIPS, TOKS, C)
            enc_grads[level][batch_idx] = pre_grad
            from_above = back_grad
    input_grads = jnp.stack([jnp.stack(outputs[level]) for level in range(N_SECTION)])
    grams = jnp.stack([jnp.stack([gram_total(enc_inputs[level], enc_grads[level]), gram_total(dec_inputs[level], dec_grads[level])]) for level in range(N_SECTION)])
    return input_grads, grams
```

```python
import jax
import jax.numpy as jnp
from jax import lax
from jax.experimental import pallas as pl
from jax.experimental.pallas import tpu as pltpu
from jax.sharding import PartitionSpec as P

MESH = pl.DeviceIdType.MESH
F32 = jnp.float32
BF16 = jnp.bfloat16

C = 1280
HALF = C // 2
ROWS = 192
PIECE = 32
PIECES = ROWS // PIECE
FRAME = 24
LEVELS = 8
BLOCK = 80
OUT_ROWS = 40
PHASES = 6
DENOM = 7864320.0
ENC, DEC = 0, 1


def kernel(
    emb_ref, enc_w, dec_w, mod_hbm, enc_u, dec_u, cot_hbm, out_ref, gram_ref,
    w, wt, mod, u, sg, chain_in, back, delta, gains,
    u4, d4, part, from_rep, from_z, g, gram_acc, own_gram, send_gram, recv_gram,
    load_sem, chain_s, chain_r, u_s, u_r, d_s, d_r, x_s, x_r, z_s, z_r,
    az_s, az_r, ax_s, ax_r, ac_s, ac_r, f_s, f_r,
):
    s = lax.axis_index("section")
    dp = lax.axis_index("dp")
    r = lax.axis_index("rep")
    z, c = dp // 2, dp % 2
    zp, zg = z % 2, z // 2
    up = {"section": lax.rem(s + 1, LEVELS)}
    down = {"section": lax.rem(s + LEVELS - 1, LEVELS)}
    z_other = z + 1 - 2 * zp
    sibling = {"dp": z * 2 + 1 - c}
    pair_same = {"dp": z_other * 2 + c}
    pair_cross = {"dp": z_other * 2 + 1 - c}
    rep_other = {"rep": 1 - r}
    quad = [sibling, pair_same, pair_cross]
    quad_core = [1 - c, c, 1 - c]
    quad_zp = [zp, 1 - zp, 1 - zp]
    zg_of = [lax.rem(zg + 1 + j, 4) for j in range(3)]
    z_group = [{"dp": (zg_of[j] * 2 + zp) * 2 + c} for j in range(3)]
    slot = zp * 2 + c
    quad_slot = [zp * 2 + 1 - c, (1 - zp) * 2 + c, (1 - zp) * 2 + 1 - c]

    def remote(src, dst, ss, rs, dev):
        return pltpu.make_async_remote_copy(
            src_ref=src, dst_ref=dst, send_sem=ss, recv_sem=rs, device_id=dev, device_id_type=MESH
        )

    def load(src, dst, a, b):
        return pltpu.make_async_copy(src, dst, load_sem.at[a, b])

    load(dec_u, u.at[DEC], DEC, 1).start()
    load(enc_u, u.at[ENC], ENC, 1).start()
    load(dec_w, w.at[DEC], DEC, 0).start()
    load(mod_hbm.at[DEC], mod.at[DEC], DEC, 2).start()
    cot_load = pltpu.make_async_copy(cot_hbm, chain_in.at[DEC], load_sem.at[0, 3])

    @pl.when(s == 0)
    def _():
        cot_load.start()

    load(enc_w, w.at[ENC], ENC, 0).start()
    load(mod_hbm.at[ENC], mod.at[ENC], ENC, 2).start()

    barrier = pltpu.get_barrier_semaphore()
    partners = [up, down, rep_other] + quad + z_group
    for dev in partners:
        pl.semaphore_signal(barrier, inc=1, device_id=dev, device_id_type=MESH)

    @pl.when(s == LEVELS - 1)
    def _():
        chain_in[ENC] = jnp.zeros((ROWS, C), BF16)

    def col(h):
        return pl.ds(pl.multiple_of(h * HALF, HALF), HALF)

    def rows(start, size, unit):
        return pl.ds(pl.multiple_of(start, unit), size)

    def prep(side):
        load(dec_w, w.at[side], side, 0).wait()
        load(mod_hbm.at[DEC], mod.at[side], side, 2).wait()
        sg[side] = jnp.dot(u[side], w[side], preferred_element_type=F32)
        e = emb_ref[...]
        hi = e.astype(BF16)
        rest = e - hi.astype(F32)
        mid = rest.astype(BF16)
        low = (rest - mid.astype(F32)).astype(BF16)
        table = mod[side]
        gains[...] = 1.0 + (
            jnp.dot(hi, table, preferred_element_type=F32)
            + (jnp.dot(mid, table, preferred_element_type=F32) + jnp.dot(low, table, preferred_element_type=F32))
        )

        def frame(f, carry):
            at = rows(f * FRAME, FRAME, 8)
            gain = gains[pl.ds(f, 1), :]
            pre = sg[side, at, :] * gain
            sigma = jax.nn.sigmoid(pre)
            sg[side, at, :] = sigma * (1.0 + pre * (1.0 - sigma)) * gain
            return carry

        lax.fori_loop(0, ROWS // FRAME, frame, 0)
        wt[side] = w[side].T

    def chain_copy(side, m):
        at = rows(m * PIECE, PIECE, PIECE)
        dev = {"section": jnp.where(side == DEC, lax.rem(s + 1, LEVELS), lax.rem(s + LEVELS - 1, LEVELS))}
        return remote(back.at[side, at], chain_in.at[side, at], chain_s.at[side, m], chain_r.at[side, m], dev)

    def delta_copy(side, m, q):
        at = rows(m * PIECE, PIECE, PIECE)
        there = rows(slot * ROWS + m * PIECE, PIECE, PIECE)
        return remote(
            delta.at[side, at, col(quad_core[q])], d4.at[side, there], d_s.at[side, q, m], d_r.at[side, q, m], quad[q]
        )

    def u_copy(side, q):
        there = rows(slot * ROWS, ROWS, ROWS)
        return remote(u.at[side, :, col(quad_zp[q])], u4.at[side, there], u_s.at[side, q], u_r.at[side, q], quad[q])

    def level(side, m, incoming):
        at = rows(m * PIECE, PIECE, PIECE)
        d = (incoming * sg[side, at, :]).astype(BF16)
        delta[side, at, :] = d
        back[side, at, :] = jnp.dot(d, wt[side], preferred_element_type=F32).astype(BF16)

    def share_delta(side, m):
        for q in range(3):
            delta_copy(side, m, q).start()
        at = rows(m * PIECE, PIECE, PIECE)
        d4[side, rows(slot * ROWS + m * PIECE, PIECE, PIECE), :] = delta[side, at, col(c)]

    def piece_rows(rr, zz):
        return rows((rr * 4 + zz) * BLOCK, BLOCK, 16)

    def x_copy(side, zz):
        return remote(
            part.at[side, piece_rows(1 - r, zz)], from_rep.at[side, rows(zz * BLOCK, BLOCK, 16)],
            x_s.at[side, zz], x_r.at[side, zz], rep_other,
        )

    def z_copy(side, j):
        return remote(
            part.at[side, piece_rows(r, zg_of[j])], from_z.at[side, 2 - j], z_s.at[side, j], z_r.at[side, 2 - j], z_group[j]
        )

    def g_piece(side, rr, zz, cc):
        return g.at[side, piece_rows(rr, zz), col(cc)]

    def az_copy(side, j):
        p = g_piece(side, r, zg, c)
        return remote(p, p, az_s.at[side, j], az_r.at[side, 2 - j], z_group[j])

    def ax_copy(side, zz):
        p = g_piece(side, r, zz, c)
        return remote(p, p, ax_s.at[side, zz], ax_r.at[side, zz], rep_other)

    def ac_copy(side, rr, zz):
        p = g_piece(side, rr, zz, c)
        return remote(p, p, ac_s.at[side, rr * 4 + zz], ac_r.at[side, rr * 4 + zz], sibling)

    def f_copy(side):
        return remote(send_gram.at[side], recv_gram.at[side], f_s.at[side], f_r.at[side], pair_same)

    def window(side, base):
        start = jnp.minimum((base // 128) * 128, C - 256)
        cols = pl.ds(pl.multiple_of(start, 128), 256)
        gram_acc[...] = lax.dot_general(
            g[side, :, cols], g[side], (((0,), (0,)), ((), ())), preferred_element_type=F32
        )
        return gram_acc[rows(base - start, OUT_ROWS, 8), :]

    def phase(p, side):
        @pl.when(p == -1)
        def _():
            prep(side)

        @pl.when(p == 0)
        def _():
            for q in range(3):
                u_copy(side, q).wait_recv()

                def one(m, carry):
                    delta_copy(side, m, q).wait_recv()
                    return carry

                lax.fori_loop(0, PIECES, one, 0)
            part[side] = lax.dot_general(
                u4[side], d4[side], (((0,), (0,)), ((), ())), preferred_element_type=F32
            ).astype(BF16)
            for j in range(3):
                x_copy(side, zg_of[j]).start()
            x_copy(side, zg).start()

        @pl.when(p == 1)
        def _():
            for j in range(3):
                x_copy(side, zg_of[j]).wait_recv()
                at = piece_rows(r, zg_of[j])
                part[side, at, :] = (
                    part[side, at, :].astype(F32)
                    + from_rep[side, rows(zg_of[j] * BLOCK, BLOCK, 16), :].astype(F32)
                ).astype(BF16)
                z_copy(side, j).start()

        @pl.when(p == 2)
        def _():
            x_copy(side, zg).wait_recv()
            total = part[side, piece_rows(r, zg), :].astype(F32) + from_rep[
                side, rows(zg * BLOCK, BLOCK, 16), :
            ].astype(F32)
            for j in range(3):
                z_copy(side, 2 - j).wait_recv()
                total = total + from_z[side, j].astype(F32)
            g[side, piece_rows(r, zg), col(c)] = total.astype(BF16)
            for j in range(3):
                az_copy(side, j).start()
            ax_copy(side, zg).start()
            ac_copy(side, r, zg).start()

        @pl.when(p == 3)
        def _():
            for j in range(3):
                zz = lax.rem(zg + 1 + j, 4)
                az_copy(side, 2 - j).wait_recv()
                ax_copy(side, zz).start()
                ac_copy(side, r, zz).start()

        @pl.when(p == 4)
        def _():
            ax_copy(side, zg).wait_recv()
            ac_copy(side, 1 - r, zg).start()
            for j in range(3):
                ax_copy(side, zg_of[j]).wait_recv()
                ac_copy(side, 1 - r, zg_of[j]).start()
            for rr in range(2):
                for zz in range(4):
                    ac_copy(side, rr, zz).wait_recv()
            send_gram[side] = window(side, 160 * z_other + 80 * c + 40 * r)
            f_copy(side).start()
            own_gram[side] = window(side, 160 * z + 80 * c + 40 * r)

        @pl.when(p == 5)
        def _():
            f_copy(side).wait_recv()
            gram_ref[side] = (own_gram[side] + recv_gram[side]) / DENOM

    early = jnp.where(
        s <= 2, PHASES, jnp.where(s == 3, 3, jnp.where(s == 4, 2, jnp.where(s == 5, 1, 0)))
    )

    def step(i, carry):
        last = s == LEVELS - 1
        is_chain = (i >= 0) & (i < 2 * PIECES)
        is_dec = is_chain & jnp.where(last, i % 2 == 0, i < PIECES)
        is_enc = is_chain & jnp.where(last, i % 2 == 1, i >= PIECES)
        m = jnp.where(last, i // 2, i % PIECES)

        @pl.when(is_dec)
        def _():
            @pl.when(s > 0)
            def _():
                chain_copy(DEC, m).wait_recv()

            @pl.when((s == 0) & (m == 0))
            def _():
                cot_load.wait()

            at = rows(m * PIECE, PIECE, PIECE)
            level(DEC, m, chain_in[DEC, at, :].astype(F32))

            @pl.when(s < LEVELS - 1)
            def _():
                chain_copy(DEC, m).start()

            share_delta(DEC, m)

        @pl.when(is_enc)
        def _():
            @pl.when(s < LEVELS - 1)
            def _():
                chain_copy(ENC, m).wait_recv()

            at = rows(m * PIECE, PIECE, PIECE)
            both = (back[DEC, at, :].astype(F32) + chain_in[ENC, at, :].astype(F32)).astype(BF16)
            level(ENC, m, both.astype(F32))

            @pl.when(s > 0)
            def _():
                chain_copy(ENC, m).start()

            share_delta(ENC, m)
            out_ref[at, :] = back[ENC, at, :]

        middle = i == PIECES - 1
        late = i >= 2 * PIECES
        n = jnp.where(middle, jnp.where(s == 0, early + 1, early), jnp.where(late, 2, 0))

        def event(j, carry):
            p = jnp.where(middle, jnp.where(s == 0, j - 1, j), i - 2 * PIECES)
            side = jnp.where(middle, jnp.where(p < 0, ENC, DEC), 1 - j)
            done = late & (side == DEC) & (p < early)

            @pl.when(jnp.logical_not(done))
            def _():
                phase(p, side)

            return carry

        lax.fori_loop(0, n, event, 0)

        return carry

    load(dec_u, u.at[DEC], DEC, 1).wait()
    load(enc_u, u.at[ENC], ENC, 1).wait()

    def prepare(j, carry):
        prep(1 - j)
        return carry

    lax.fori_loop(0, jnp.where(s == 0, 1, 2), prepare, 0)
    pl.semaphore_wait(barrier, len(partners))
    for side in (DEC, ENC):
        for q in range(3):
            u_copy(side, q).start()
        u4[side, rows(slot * ROWS, ROWS, ROWS), :] = u[side, :, col(zp)]
    lax.fori_loop(0, 2 * PIECES + PHASES, step, 0)

    for side in (DEC, ENC):
        for q in range(3):
            u_copy(side, q).wait_send()

            def sent(m, carry):
                delta_copy(side, m, q).wait_send()
                return carry

            lax.fori_loop(0, PIECES, sent, 0)

        def chained(m, carry):
            chain_copy(side, m).wait_send()
            return carry

        @pl.when((s < LEVELS - 1) if side == DEC else (s > 0))
        def _():
            lax.fori_loop(0, PIECES, chained, 0)

        for j in range(3):
            z_copy(side, j).wait_send()
            az_copy(side, j).wait_send()
        for zz in range(4):
            x_copy(side, zz).wait_send()
            ax_copy(side, zz).wait_send()
            for rr in range(2):
                ac_copy(side, rr, zz).wait_send()
        f_copy(side).wait_send()


def body(enc_weight, dec_weight, modulation, enc_inputs, dec_inputs, cotangent, timesteps):
    half = modulation.shape[2] // 2
    freqs = jnp.exp(-jnp.log(10000.0) * jnp.arange(half).astype(F32) / half)
    angles = timesteps.reshape(-1).astype(F32)[:, None] * freqs
    emb = jnp.concatenate([jnp.sin(angles), jnp.cos(angles)], axis=-1)
    dma = pltpu.SemaphoreType.DMA
    out, grams = pl.pallas_call(
        kernel,
        name="unet_backward",
        out_shape=(jax.ShapeDtypeStruct((ROWS, C), BF16), jax.ShapeDtypeStruct((2, OUT_ROWS, C), F32)),
        in_specs=[pl.BlockSpec(memory_space=pltpu.VMEM)] + [pl.BlockSpec(memory_space=pl.ANY)] * 6,
        out_specs=(pl.BlockSpec(memory_space=pltpu.VMEM), pl.BlockSpec(memory_space=pltpu.VMEM)),
        scratch_shapes=[
            pltpu.VMEM((2, C, C), BF16), pltpu.VMEM((2, C, C), BF16), pltpu.VMEM((2, 256, C), BF16),
            pltpu.VMEM((2, ROWS, C), BF16), pltpu.VMEM((2, ROWS, C), F32), pltpu.VMEM((2, ROWS, C), BF16),
            pltpu.VMEM((2, ROWS, C), BF16), pltpu.VMEM((2, ROWS, C), BF16), pltpu.VMEM((8, C), F32),
            pltpu.VMEM((2, 4 * ROWS, HALF), BF16), pltpu.VMEM((2, 4 * ROWS, HALF), BF16),
            pltpu.VMEM((2, HALF, HALF), BF16), pltpu.VMEM((2, HALF // 2, HALF), BF16),
            pltpu.VMEM((2, 3, BLOCK, HALF), BF16), pltpu.VMEM((2, HALF, C), BF16), pltpu.VMEM((256, C), F32),
            pltpu.VMEM((2, OUT_ROWS, C), F32), pltpu.VMEM((2, OUT_ROWS, C), F32), pltpu.VMEM((2, OUT_ROWS, C), F32),
            dma((2, 4)), dma((2, PIECES)), dma((2, PIECES)), dma((2, 3)), dma((2, 3)),
            dma((2, 3, PIECES)), dma((2, 3, PIECES)), dma((2, 4)), dma((2, 4)), dma((2, 3)), dma((2, 3)),
            dma((2, 3)), dma((2, 3)), dma((2, 4)), dma((2, 4)), dma((2, 8)), dma((2, 8)), dma((2,)), dma((2,)),
        ],
        compiler_params=pltpu.CompilerParams(
            collective_id=0, has_side_effects=True, vmem_limit_bytes=60 * 1024 * 1024
        ),
    )(
        emb, enc_weight.reshape(C, C), dec_weight.reshape(C, C), modulation.reshape(2, 256, C),
        enc_inputs.reshape(ROWS, C), dec_inputs.reshape(ROWS, C), cotangent.reshape(ROWS, C),
    )
    return out.reshape(1, 2, 1, ROWS // 2, C), grams[None]


def solution(mesh):
    return jax.shard_map(
        body,
        mesh=mesh,
        in_specs=(
            P("section", None, None),
            P("section", None, None),
            P("section", None, None, None),
            P("section", None, ("dp", "rep"), None, None),
            P("section", None, ("dp", "rep"), None, None),
            P(None, ("dp", "rep"), None, None),
            P(None, ("dp", "rep"), None),
        ),
        out_specs=(
            P("section", None, ("dp", "rep"), None, None),
            P("section", None, ("dp", "rep"), None),
        ),
        check_vma=False,
    )
```

```python
import jax
import jax.numpy as jnp
from jax import lax
from jax.experimental import pallas as pl
from jax.experimental.pallas import tpu as pltpu
from jax.sharding import PartitionSpec as P

MESH = pl.DeviceIdType.MESH
F32 = jnp.float32
BF16 = jnp.bfloat16

C = 1280
HALF = C // 2
ROWS = 192
PIECE = 32
PIECES = ROWS // PIECE
SPLIT = 2
PART = C // SPLIT
FRAME = 24
LEVELS = 8
BLOCK = 80
OUT_ROWS = 40
PHASES = 7
EARLY = (6, 6, 5, 4, 2, 2, 1, 1)
DENOM = 7864320.0
ENC, DEC = 0, 1


def kernel(
    emb_ref, enc_w, dec_w, mod_hbm, enc_u, dec_u, cot_hbm, out_ref, gram_ref,
    w, wt, mod, u, sg, chain_in, back, delta, gains,
    u4, u4t, d4, part, from_rep, from_z, g, gram_acc, own_gram, send_gram, recv_gram,
    load_sem, chain_s, chain_r, u_s, u_r, d_s, d_r, x_s, x_r, z_s, z_r,
    az_s, az_r, ac_s, ac_r, f_s, f_r,
):
    s = lax.axis_index("section")
    dp = lax.axis_index("dp")
    r = lax.axis_index("rep")
    z, c = dp // 2, dp % 2
    zp, zg = z % 2, z // 2
    up = {"section": lax.rem(s + 1, LEVELS)}
    down = {"section": lax.rem(s + LEVELS - 1, LEVELS)}
    z_other = z + 1 - 2 * zp
    sibling = {"dp": z * 2 + 1 - c}
    pair_same = {"dp": z_other * 2 + c}
    pair_cross = {"dp": z_other * 2 + 1 - c}
    rep_other = {"rep": 1 - r}
    quad = [sibling, pair_same, pair_cross]
    quad_core = [1 - c, c, 1 - c]
    quad_zp = [zp, 1 - zp, 1 - zp]
    zg_of = [lax.rem(zg + 1 + j, 4) for j in range(3)]
    z_group = [{"dp": (zg_of[j] * 2 + zp) * 2 + c} for j in range(3)]
    gram_peer = [{"dp": z_other * 2 + c, "rep": 1 - r}, pair_same, rep_other]
    slot = zp * 2 + c
    quad_slot = [zp * 2 + 1 - c, (1 - zp) * 2 + c, (1 - zp) * 2 + 1 - c]

    def remote(src, dst, ss, rs, dev):
        return pltpu.make_async_remote_copy(
            src_ref=src, dst_ref=dst, send_sem=ss, recv_sem=rs, device_id=dev, device_id_type=MESH
        )

    def load(src, dst, a, b):
        return pltpu.make_async_copy(src, dst, load_sem.at[a, b])

    load(dec_u, u.at[DEC], DEC, 1).start()
    load(enc_u, u.at[ENC], ENC, 1).start()
    load(dec_w, w.at[DEC], DEC, 0).start()
    load(mod_hbm.at[DEC], mod.at[DEC], DEC, 2).start()
    cot_load = pltpu.make_async_copy(cot_hbm, chain_in.at[DEC], load_sem.at[0, 3])

    @pl.when(s == 0)
    def _():
        cot_load.start()

    load(enc_w, w.at[ENC], ENC, 0).start()
    load(mod_hbm.at[ENC], mod.at[ENC], ENC, 2).start()

    barrier = pltpu.get_barrier_semaphore()
    partners = [up, down, gram_peer[0], rep_other] + quad + z_group
    for dev in partners:
        pl.semaphore_signal(barrier, inc=1, device_id=dev, device_id_type=MESH)

    @pl.when(s == LEVELS - 1)
    def _():
        chain_in[ENC] = jnp.zeros((ROWS, C), BF16)

    def col(h):
        return pl.ds(pl.multiple_of(h * HALF, HALF), HALF)

    def rows(start, size, unit):
        return pl.ds(pl.multiple_of(start, unit), size)

    def prep(side):
        load(dec_w, w.at[side], side, 0).wait()
        load(mod_hbm.at[DEC], mod.at[side], side, 2).wait()
        sg[side] = jnp.dot(u[side], w[side], preferred_element_type=F32)
        e = emb_ref[...]
        hi = e.astype(BF16)
        rest = e - hi.astype(F32)
        mid = rest.astype(BF16)
        low = (rest - mid.astype(F32)).astype(BF16)
        table = mod[side]
        gains[...] = 1.0 + (
            jnp.dot(hi, table, preferred_element_type=F32)
            + (jnp.dot(mid, table, preferred_element_type=F32) + jnp.dot(low, table, preferred_element_type=F32))
        )

        def frame(f, carry):
            at = rows(f * FRAME, FRAME, 8)
            gain = gains[pl.ds(f, 1), :]
            pre = sg[side, at, :] * gain
            sigma = jax.nn.sigmoid(pre)
            sg[side, at, :] = sigma * (1.0 + pre * (1.0 - sigma)) * gain
            return carry

        lax.fori_loop(0, ROWS // FRAME, frame, 0)
        wt[side] = w[side].T

    def chain_copy(side, m, k):
        at = rows(m * PIECE, PIECE, PIECE)
        cols = pl.ds(k * PART, PART)
        dev = {"section": jnp.where(side == DEC, lax.rem(s + 1, LEVELS), lax.rem(s + LEVELS - 1, LEVELS))}
        return remote(
            back.at[side, at, cols], chain_in.at[side, at, cols], chain_s.at[side, m, k], chain_r.at[side, m, k], dev
        )

    def delta_copy(side, m, q):
        at = rows(m * PIECE, PIECE, PIECE)
        there = rows(slot * ROWS + m * PIECE, PIECE, PIECE)
        return remote(
            delta.at[side, at, col(quad_core[q])], d4.at[side, there], d_s.at[side, q, m], d_r.at[side, q, m], quad[q]
        )

    def u_copy(side, q):
        there = rows(slot * ROWS, ROWS, ROWS)
        return remote(u.at[side, :, col(quad_zp[q])], u4.at[side, there], u_s.at[side, q], u_r.at[side, q], quad[q])

    def level(side, m, incoming, sends):
        at = rows(m * PIECE, PIECE, PIECE)
        d = (incoming * sg[side, at, :]).astype(BF16)
        delta[side, at, :] = d
        for k in range(SPLIT):
            cols = pl.ds(k * PART, PART)
            back[side, at, cols] = jnp.dot(d, wt[side, :, cols], preferred_element_type=F32).astype(BF16)

            @pl.when(sends)
            def _():
                chain_copy(side, m, k).start()

    def share_delta(side, m):
        for q in range(3):
            delta_copy(side, m, q).start()
        at = rows(m * PIECE, PIECE, PIECE)
        d4[side, rows(slot * ROWS + m * PIECE, PIECE, PIECE), :] = delta[side, at, col(c)]

    def piece_rows(rr, zz):
        return rows((rr * 4 + zz) * BLOCK, BLOCK, 16)

    def x_copy(side, zz):
        return remote(
            part.at[side, piece_rows(1 - r, zz)], from_rep.at[side, rows(zz * BLOCK, BLOCK, 16)],
            x_s.at[side, zz], x_r.at[side, zz], rep_other,
        )

    def z_copy(side, j):
        return remote(
            part.at[side, piece_rows(r, zg_of[j])], from_z.at[side, 2 - j], z_s.at[side, j], z_r.at[side, 2 - j], z_group[j]
        )

    def g_piece(side, zz):
        return g.at[side, rows(zz * BLOCK, BLOCK, 16), col(c)]

    def az_copy(side, j):
        p = g_piece(side, zg)
        return remote(p, p, az_s.at[side, j], az_r.at[side, 2 - j], z_group[j])

    def ac_copy(side, zz):
        p = g_piece(side, zz)
        return remote(p, p, ac_s.at[side, zz], ac_r.at[side, zz], sibling)

    def f_copy(side, j):
        return remote(send_gram.at[side, j], recv_gram.at[side, j], f_s.at[side, j], f_r.at[side, j], gram_peer[j])

    def multiply_gathered(side, zz):
        base = 160 * zz + 80 * c
        start = jnp.minimum((base // 128) * 128, C - 256)
        cols = pl.ds(pl.multiple_of(start, 128), 256)
        gram_acc[...] = lax.dot_general(
            g[side, :, cols], g[side], (((0,), (0,)), ((), ())), preferred_element_type=F32
        )
        return base - start

    def phase(p, side):
        @pl.when(p == -1)
        def _():
            prep(side)

        @pl.when(p == 0)
        def _():
            for q in range(3):
                u_copy(side, q).wait_recv()
            u4t[side] = u4[side].T

        @pl.when(p == 1)
        def _():
            for q in range(3):

                def one(m, carry):
                    delta_copy(side, m, q).wait_recv()
                    return carry

                lax.fori_loop(0, PIECES, one, 0)
            for rr in (1 - r, r):
                at = rows(rr * (HALF // 2), HALF // 2, 16)
                part[side, at, :] = jnp.dot(
                    u4t[side, at, :], d4[side], preferred_element_type=F32
                ).astype(BF16)
                if rr is not r:
                    for j in range(3):
                        x_copy(side, zg_of[j]).start()
                    x_copy(side, zg).start()

        @pl.when(p == 2)
        def _():
            for j in range(3):
                x_copy(side, zg_of[j]).wait_recv()
                at = piece_rows(r, zg_of[j])
                part[side, at, :] = (
                    part[side, at, :].astype(F32)
                    + from_rep[side, rows(zg_of[j] * BLOCK, BLOCK, 16), :].astype(F32)
                ).astype(BF16)
                z_copy(side, j).start()

        @pl.when(p == 3)
        def _():
            x_copy(side, zg).wait_recv()
            total = part[side, piece_rows(r, zg), :].astype(F32) + from_rep[
                side, rows(zg * BLOCK, BLOCK, 16), :
            ].astype(F32)
            for j in range(3):
                z_copy(side, 2 - j).wait_recv()
                total = total + from_z[side, j].astype(F32)
            g[side, rows(zg * BLOCK, BLOCK, 16), col(c)] = total.astype(BF16)
            for j in range(3):
                az_copy(side, j).start()
            ac_copy(side, zg).start()

        @pl.when(p == 4)
        def _():
            for j in range(3):
                az_copy(side, 2 - j).wait_recv()
                ac_copy(side, zg_of[j]).start()

        @pl.when(p == 5)
        def _():
            for zz in range(4):
                ac_copy(side, zz).wait_recv()

            def there(k, carry):
                offset = multiply_gathered(side, jnp.where(k == 0, z_other, z))

                @pl.when(k == 0)
                def _():
                    for j, rr in ((0, 1 - r), (1, r)):
                        send_gram[side, j] = gram_acc[rows(offset + 40 * rr, OUT_ROWS, 8), :].astype(BF16)
                        f_copy(side, j).start()

                @pl.when(k == 1)
                def _():
                    send_gram[side, 2] = gram_acc[rows(offset + 40 * (1 - r), OUT_ROWS, 8), :].astype(BF16)
                    f_copy(side, 2).start()
                    own_gram[side] = gram_acc[rows(offset + 40 * r, OUT_ROWS, 8), :]

                return carry

            lax.fori_loop(0, 2, there, 0)

        @pl.when(p == 6)
        def _():
            gram = own_gram[side]
            for j in range(3):
                f_copy(side, j).wait_recv()
                gram = gram + recv_gram[side, j].astype(F32)
            gram_ref[side] = gram / DENOM

    early = jnp.int32(0)
    for level_index, count in enumerate(EARLY):
        early = jnp.where(s == level_index, count, early)

    def step(t, carry):
        i = jnp.maximum(t, 1) - 1
        last = s == LEVELS - 1
        is_chain = (t > 0) & (t <= 2 * PIECES)
        is_dec = is_chain & jnp.where(last, i % 2 == 0, i < PIECES)
        is_enc = is_chain & jnp.where(last, i % 2 == 1, i >= PIECES)
        m = jnp.where(last, lax.div(i, 2), lax.rem(i, PIECES))

        @pl.when(is_dec)
        def _():
            @pl.when(s > 0)
            def _():
                for k in range(SPLIT):
                    chain_copy(DEC, m, k).wait_recv()

            @pl.when((s == 0) & (m == 0))
            def _():
                cot_load.wait()

            at = rows(m * PIECE, PIECE, PIECE)
            level(DEC, m, chain_in[DEC, at, :].astype(F32), s < LEVELS - 1)
            share_delta(DEC, m)

        @pl.when(is_enc)
        def _():
            @pl.when(s < LEVELS - 1)
            def _():
                for k in range(SPLIT):
                    chain_copy(ENC, m, k).wait_recv()

            at = rows(m * PIECE, PIECE, PIECE)
            both = (back[DEC, at, :].astype(F32) + chain_in[ENC, at, :].astype(F32)).astype(BF16)
            level(ENC, m, both.astype(F32), s > 0)
            share_delta(ENC, m)
            out_ref[at, :] = back[ENC, at, :]

        first = t == 0
        middle = t == PIECES
        late = t > 2 * PIECES
        front = s < 4
        lead = jnp.where(s == 0, 2, 1)
        n = jnp.where(
            first,
            jnp.where(front, 0, 2),
            jnp.where(middle, jnp.where(front, lead + early, early - 1), jnp.where(late, 2, 0)),
        )

        def event(j, carry):
            p_middle = jnp.where(front, jnp.where(j < lead, j + 1 - lead, j - lead), j + 1)
            p = jnp.where(first, 0, jnp.where(middle, p_middle, t - 2 * PIECES))
            side = jnp.where(middle, jnp.where(front & (j < lead), ENC, DEC), 1 - j)
            done = late & (side == DEC) & (p < early)

            @pl.when(jnp.logical_not(done))
            def _():
                phase(p, side)

            return carry

        lax.fori_loop(0, n, event, 0)

        return carry

    load(dec_u, u.at[DEC], DEC, 1).wait()
    load(enc_u, u.at[ENC], ENC, 1).wait()

    def prepare(j, carry):
        prep(1 - j)
        return carry

    lax.fori_loop(0, jnp.where(s == 0, 1, 2), prepare, 0)
    pl.semaphore_wait(barrier, len(partners))
    for side in (DEC, ENC):
        for q in range(3):
            u_copy(side, q).start()
        u4[side, rows(slot * ROWS, ROWS, ROWS), :] = u[side, :, col(zp)]
    lax.fori_loop(0, 2 * PIECES + PHASES, step, 0)

    for side in (DEC, ENC):
        for q in range(3):
            u_copy(side, q).wait_send()

            def sent(m, carry):
                delta_copy(side, m, q).wait_send()
                return carry

            lax.fori_loop(0, PIECES, sent, 0)

        def chained(m, carry):
            for k in range(SPLIT):
                chain_copy(side, m, k).wait_send()
            return carry

        @pl.when((s < LEVELS - 1) if side == DEC else (s > 0))
        def _():
            lax.fori_loop(0, PIECES, chained, 0)

        for j in range(3):
            z_copy(side, j).wait_send()
            az_copy(side, j).wait_send()
            f_copy(side, j).wait_send()
        for zz in range(4):
            x_copy(side, zz).wait_send()
            ac_copy(side, zz).wait_send()


def body(enc_weight, dec_weight, modulation, enc_inputs, dec_inputs, cotangent, timesteps):
    half = modulation.shape[2] // 2
    freqs = jnp.exp(-jnp.log(10000.0) * jnp.arange(half).astype(F32) / half)
    angles = timesteps.reshape(-1).astype(F32)[:, None] * freqs
    emb = jnp.concatenate([jnp.sin(angles), jnp.cos(angles)], axis=-1)
    dma = pltpu.SemaphoreType.DMA
    out, grams = pl.pallas_call(
        kernel,
        name="unet_backward",
        out_shape=(jax.ShapeDtypeStruct((ROWS, C), BF16), jax.ShapeDtypeStruct((2, OUT_ROWS, C), F32)),
        in_specs=[pl.BlockSpec(memory_space=pltpu.VMEM)] + [pl.BlockSpec(memory_space=pl.ANY)] * 6,
        out_specs=(pl.BlockSpec(memory_space=pltpu.VMEM), pl.BlockSpec(memory_space=pltpu.VMEM)),
        scratch_shapes=[
            pltpu.VMEM((2, C, C), BF16), pltpu.VMEM((2, C, C), BF16), pltpu.VMEM((2, 256, C), BF16),
            pltpu.VMEM((2, ROWS, C), BF16), pltpu.VMEM((2, ROWS, C), F32), pltpu.VMEM((2, ROWS, C), BF16),
            pltpu.VMEM((2, ROWS, C), BF16), pltpu.VMEM((2, ROWS, C), BF16), pltpu.VMEM((8, C), F32),
            pltpu.VMEM((2, 4 * ROWS, HALF), BF16), pltpu.VMEM((2, HALF, 4 * ROWS), BF16),
            pltpu.VMEM((2, 4 * ROWS, HALF), BF16),
            pltpu.VMEM((2, HALF, HALF), BF16), pltpu.VMEM((2, HALF // 2, HALF), BF16),
            pltpu.VMEM((2, 3, BLOCK, HALF), BF16), pltpu.VMEM((2, HALF // 2, C), BF16), pltpu.VMEM((256, C), F32),
            pltpu.VMEM((2, OUT_ROWS, C), F32), pltpu.VMEM((2, 3, OUT_ROWS, C), BF16),
            pltpu.VMEM((2, 3, OUT_ROWS, C), BF16),
            dma((2, 4)), dma((2, PIECES, SPLIT)), dma((2, PIECES, SPLIT)), dma((2, 3)), dma((2, 3)),
            dma((2, 3, PIECES)), dma((2, 3, PIECES)), dma((2, 4)), dma((2, 4)), dma((2, 3)), dma((2, 3)),
            dma((2, 3)), dma((2, 3)), dma((2, 4)), dma((2, 4)), dma((2, 3)), dma((2, 3)),
        ],
        compiler_params=pltpu.CompilerParams(
            collective_id=0, has_side_effects=True, vmem_limit_bytes=40 * 1024 * 1024
        ),
    )(
        emb, *[pltpu.with_memory_space_constraint(a, pltpu.HBM) for a in (enc_weight.reshape(C, C), dec_weight.reshape(C, C), modulation.reshape(2, 256, C),
        enc_inputs.reshape(ROWS, C), dec_inputs.reshape(ROWS, C), cotangent.reshape(ROWS, C))],
    )
    return out.reshape(1, 2, 1, ROWS // 2, C), grams[None]


def solution(mesh):
    return jax.shard_map(
        body,
        mesh=mesh,
        in_specs=(
            P("section", None, None),
            P("section", None, None),
            P("section", None, None, None),
            P("section", None, ("dp", "rep"), None, None),
            P("section", None, ("dp", "rep"), None, None),
            P(None, ("dp", "rep"), None, None),
            P(None, ("dp", "rep"), None),
        ),
        out_specs=(
            P("section", None, ("dp", "rep"), None, None),
            P("section", None, ("dp", "rep"), None),
        ),
        check_vma=False,
    )
```

```python
import jax
import jax.numpy as jnp
from jax import lax
from jax.experimental import pallas as pl
from jax.experimental.pallas import tpu as pltpu
from jax.sharding import PartitionSpec as P

MESH = pl.DeviceIdType.MESH
F32 = jnp.float32
BF16 = jnp.bfloat16

C = 1280
HALF = C // 2
ROWS = 192
PIECE = 32
PIECES = ROWS // PIECE
SPLIT = 2
PART = C // SPLIT
FRAME = 24
LEVELS = 8
BLOCK = 80
OUT_ROWS = 40
PHASES = 6
EARLY = (3, 3, 3, 1, 1, 0, 0, 0)
DENOM = 7864320.0
ENC, DEC = 0, 1


def kernel(
    emb_ref, enc_w, dec_w, mod_hbm, enc_u, dec_u, cot_hbm, out_ref, gram_ref,
    w, wt, mod, u, sg, chain_in, back, delta, gains,
    u4, d4, part, from_rep, from_z, g, gram_acc, own_gram, send_gram, recv_gram,
    load_sem, chain_s, chain_r, u_s, u_r, d_s, d_r, x_s, x_r, z_s, z_r,
    az_s, az_r, ac_s, ac_r, f_s, f_r,
):
    s = lax.axis_index("section")
    dp = lax.axis_index("dp")
    r = lax.axis_index("rep")
    z, c = dp // 2, dp % 2
    zp, zg = z % 2, z // 2
    up = {"section": lax.rem(s + 1, LEVELS)}
    down = {"section": lax.rem(s + LEVELS - 1, LEVELS)}
    z_other = z + 1 - 2 * zp
    sibling = {"dp": z * 2 + 1 - c}
    pair_same = {"dp": z_other * 2 + c}
    pair_cross = {"dp": z_other * 2 + 1 - c}
    rep_other = {"rep": 1 - r}
    quad = [sibling, pair_same, pair_cross]
    quad_core = [1 - c, c, 1 - c]
    quad_zp = [zp, 1 - zp, 1 - zp]
    zg_of = [lax.rem(zg + 1 + j, 4) for j in range(3)]
    z_group = [{"dp": (zg_of[j] * 2 + zp) * 2 + c} for j in range(3)]
    gram_peer = [{"dp": z_other * 2 + c, "rep": 1 - r}, pair_same, rep_other]
    slot = zp * 2 + c
    quad_slot = [zp * 2 + 1 - c, (1 - zp) * 2 + c, (1 - zp) * 2 + 1 - c]

    def remote(src, dst, ss, rs, dev):
        return pltpu.make_async_remote_copy(
            src_ref=src, dst_ref=dst, send_sem=ss, recv_sem=rs, device_id=dev, device_id_type=MESH
        )

    def load(src, dst, a, b):
        return pltpu.make_async_copy(src, dst, load_sem.at[a, b])

    load(dec_u, u.at[DEC], DEC, 1).start()
    load(enc_u, u.at[ENC], ENC, 1).start()
    load(dec_w, w.at[DEC], DEC, 0).start()
    load(mod_hbm.at[DEC], mod.at[DEC], DEC, 2).start()
    cot_load = pltpu.make_async_copy(cot_hbm, chain_in.at[DEC], load_sem.at[0, 3])

    @pl.when(s == 0)
    def _():
        cot_load.start()

    load(enc_w, w.at[ENC], ENC, 0).start()
    load(mod_hbm.at[ENC], mod.at[ENC], ENC, 2).start()

    barrier = pltpu.get_barrier_semaphore()
    partners = [up, down, gram_peer[0], rep_other] + quad + z_group
    for dev in partners:
        pl.semaphore_signal(barrier, inc=1, device_id=dev, device_id_type=MESH)

    @pl.when(s == LEVELS - 1)
    def _():
        chain_in[ENC] = jnp.zeros((ROWS, C), BF16)

    def col(h):
        return pl.ds(pl.multiple_of(h * HALF, HALF), HALF)

    def rows(start, size, unit):
        return pl.ds(pl.multiple_of(start, unit), size)

    def prep(side):
        load(dec_w, w.at[side], side, 0).wait()
        load(mod_hbm.at[DEC], mod.at[side], side, 2).wait()
        sg[side] = jnp.dot(u[side], w[side], preferred_element_type=F32)
        e = emb_ref[...]
        hi = e.astype(BF16)
        rest = e - hi.astype(F32)
        mid = rest.astype(BF16)
        low = (rest - mid.astype(F32)).astype(BF16)
        table = mod[side]
        gains[...] = 1.0 + (
            jnp.dot(hi, table, preferred_element_type=F32)
            + (jnp.dot(mid, table, preferred_element_type=F32) + jnp.dot(low, table, preferred_element_type=F32))
        )

        def frame(f, carry):
            at = rows(f * FRAME, FRAME, 8)
            gain = gains[pl.ds(f, 1), :]
            pre = sg[side, at, :] * gain
            sigma = jax.nn.sigmoid(pre)
            sg[side, at, :] = sigma * (1.0 + pre * (1.0 - sigma)) * gain
            return carry

        lax.fori_loop(0, ROWS // FRAME, frame, 0)
        wt[side] = w[side].T

    def chain_copy(side, m, k):
        at = rows(m * PIECE, PIECE, PIECE)
        cols = pl.ds(k * PART, PART)
        dev = {"section": jnp.where(side == DEC, lax.rem(s + 1, LEVELS), lax.rem(s + LEVELS - 1, LEVELS))}
        return remote(
            back.at[side, at, cols], chain_in.at[side, at, cols], chain_s.at[side, m, k], chain_r.at[side, m, k], dev
        )

    def delta_copy(side, m, q):
        at = rows(m * PIECE, PIECE, PIECE)
        there = rows(slot * ROWS + m * PIECE, PIECE, PIECE)
        return remote(
            delta.at[side, at, col(quad_core[q])], d4.at[side, there], d_s.at[side, q, m], d_r.at[side, q, m], quad[q]
        )

    def u_copy(side, q):
        there = rows(slot * ROWS, ROWS, ROWS)
        return remote(u.at[side, :, col(quad_zp[q])], u4.at[side, there], u_s.at[side, q], u_r.at[side, q], quad[q])

    def level(side, m, incoming, sends):
        at = rows(m * PIECE, PIECE, PIECE)
        d = (incoming * sg[side, at, :]).astype(BF16)
        delta[side, at, :] = d
        for k in range(SPLIT):
            cols = pl.ds(k * PART, PART)
            back[side, at, cols] = jnp.dot(d, wt[side, :, cols], preferred_element_type=F32).astype(BF16)

            @pl.when(sends)
            def _():
                chain_copy(side, m, k).start()

    def share_delta(side, m):
        for q in range(3):
            delta_copy(side, m, q).start()
        at = rows(m * PIECE, PIECE, PIECE)
        d4[side, rows(slot * ROWS + m * PIECE, PIECE, PIECE), :] = delta[side, at, col(c)]

    def piece_rows(rr, zz):
        return rows((rr * 4 + zz) * BLOCK, BLOCK, 16)

    def x_copy(side, zz):
        return remote(
            part.at[side, piece_rows(1 - r, zz)], from_rep.at[side, rows(zz * BLOCK, BLOCK, 16)],
            x_s.at[side, zz], x_r.at[side, zz], rep_other,
        )

    def z_copy(side, j):
        return remote(
            part.at[side, piece_rows(r, zg_of[j])], from_z.at[side, 2 - j], z_s.at[side, j], z_r.at[side, 2 - j], z_group[j]
        )

    def g_piece(side, zz):
        return g.at[side, rows(zz * BLOCK, BLOCK, 16), col(c)]

    def az_copy(side, j):
        p = g_piece(side, zg)
        return remote(p, p, az_s.at[side, j], az_r.at[side, 2 - j], z_group[j])

    def ac_copy(side, zz):
        p = g_piece(side, zz)
        return remote(p, p, ac_s.at[side, zz], ac_r.at[side, zz], sibling)

    def f_copy(side, j):
        return remote(send_gram.at[side, j], recv_gram.at[side, j], f_s.at[side, j], f_r.at[side, j], gram_peer[j])

    def multiply_gathered(side, zz):
        base = 160 * zz + 80 * c
        start = jnp.minimum((base // 128) * 128, C - 256)
        cols = pl.ds(pl.multiple_of(start, 128), 256)
        gram_acc[...] = lax.dot_general(
            g[side, :, cols], g[side], (((0,), (0,)), ((), ())), preferred_element_type=F32
        )
        return base - start

    def phase(p, side):
        @pl.when(p == -1)
        def _():
            prep(side)

        @pl.when(p == 0)
        def _():
            for q in range(3):
                u_copy(side, q).wait_recv()

                def one(m, carry):
                    delta_copy(side, m, q).wait_recv()
                    return carry

                lax.fori_loop(0, PIECES, one, 0)
            part[side] = lax.dot_general(
                u4[side], d4[side], (((0,), (0,)), ((), ())), preferred_element_type=F32
            ).astype(BF16)
            for j in range(3):
                x_copy(side, zg_of[j]).start()
            x_copy(side, zg).start()

        @pl.when(p == 1)
        def _():
            for j in range(3):
                x_copy(side, zg_of[j]).wait_recv()
                at = piece_rows(r, zg_of[j])
                part[side, at, :] = (
                    part[side, at, :].astype(F32)
                    + from_rep[side, rows(zg_of[j] * BLOCK, BLOCK, 16), :].astype(F32)
                ).astype(BF16)
                z_copy(side, j).start()

        @pl.when(p == 2)
        def _():
            x_copy(side, zg).wait_recv()
            total = part[side, piece_rows(r, zg), :].astype(F32) + from_rep[
                side, rows(zg * BLOCK, BLOCK, 16), :
            ].astype(F32)
            for j in range(3):
                z_copy(side, 2 - j).wait_recv()
                total = total + from_z[side, j].astype(F32)
            g[side, rows(zg * BLOCK, BLOCK, 16), col(c)] = total.astype(BF16)
            for j in range(3):
                az_copy(side, j).start()
            ac_copy(side, zg).start()

        @pl.when(p == 3)
        def _():
            for j in range(3):
                az_copy(side, 2 - j).wait_recv()
                ac_copy(side, zg_of[j]).start()

        @pl.when(p == 4)
        def _():
            for zz in range(4):
                ac_copy(side, zz).wait_recv()

            def there(k, carry):
                offset = multiply_gathered(side, jnp.where(k == 0, z_other, z))

                @pl.when(k == 0)
                def _():
                    for j, rr in ((0, 1 - r), (1, r)):
                        send_gram[side, j] = gram_acc[rows(offset + 40 * rr, OUT_ROWS, 8), :].astype(BF16)
                        f_copy(side, j).start()

                @pl.when(k == 1)
                def _():
                    send_gram[side, 2] = gram_acc[rows(offset + 40 * (1 - r), OUT_ROWS, 8), :].astype(BF16)
                    f_copy(side, 2).start()
                    own_gram[side] = gram_acc[rows(offset + 40 * r, OUT_ROWS, 8), :]

                return carry

            lax.fori_loop(0, 2, there, 0)

        @pl.when(p == 5)
        def _():
            gram = own_gram[side]
            for j in range(3):
                f_copy(side, j).wait_recv()
                gram = gram + recv_gram[side, j].astype(F32)
            gram_ref[side] = gram / DENOM

    early = jnp.int32(0)
    for level_index, count in enumerate(EARLY):
        early = jnp.where(s == level_index, count, early)

    def step(i, carry):
        last = s == LEVELS - 1
        is_chain = i < 2 * PIECES
        is_dec = is_chain & jnp.where(last, i % 2 == 0, i < PIECES)
        is_enc = is_chain & jnp.where(last, i % 2 == 1, i >= PIECES)
        m = jnp.where(last, lax.div(i, 2), lax.rem(i, PIECES))

        @pl.when(is_dec)
        def _():
            @pl.when(s > 0)
            def _():
                for k in range(SPLIT):
                    chain_copy(DEC, m, k).wait_recv()

            @pl.when((s == 0) & (m == 0))
            def _():
                cot_load.wait()

            at = rows(m * PIECE, PIECE, PIECE)
            level(DEC, m, chain_in[DEC, at, :].astype(F32), s < LEVELS - 1)
            share_delta(DEC, m)

        @pl.when(is_enc)
        def _():
            @pl.when(s < LEVELS - 1)
            def _():
                for k in range(SPLIT):
                    chain_copy(ENC, m, k).wait_recv()

            at = rows(m * PIECE, PIECE, PIECE)
            both = (back[DEC, at, :].astype(F32) + chain_in[ENC, at, :].astype(F32)).astype(BF16)
            level(ENC, m, both.astype(F32), s > 0)
            share_delta(ENC, m)
            out_ref[at, :] = back[ENC, at, :]

        middle = i == PIECES - 1
        late = i >= 2 * PIECES
        lead = jnp.where(s == 0, 1, 0)
        n = jnp.where(middle, lead + early, jnp.where(late, 2, 0))

        def event(j, carry):
            p = jnp.where(middle, j - lead, i - 2 * PIECES)
            side = jnp.where(middle, jnp.where(p < 0, ENC, DEC), 1 - j)
            done = late & (side == DEC) & (p < early)

            @pl.when(jnp.logical_not(done))
            def _():
                phase(p, side)

            return carry

        lax.fori_loop(0, n, event, 0)

        return carry

    load(dec_u, u.at[DEC], DEC, 1).wait()
    load(enc_u, u.at[ENC], ENC, 1).wait()

    def prepare(j, carry):
        prep(1 - j)
        return carry

    lax.fori_loop(0, jnp.where(s == 0, 1, 2), prepare, 0)
    pl.semaphore_wait(barrier, len(partners))
    for side in (DEC, ENC):
        for q in range(3):
            u_copy(side, q).start()
        u4[side, rows(slot * ROWS, ROWS, ROWS), :] = u[side, :, col(zp)]
    lax.fori_loop(0, 2 * PIECES + PHASES, step, 0)

    for side in (DEC, ENC):
        for q in range(3):
            u_copy(side, q).wait_send()

            def sent(m, carry):
                delta_copy(side, m, q).wait_send()
                return carry

            lax.fori_loop(0, PIECES, sent, 0)

        def chained(m, carry):
            for k in range(SPLIT):
                chain_copy(side, m, k).wait_send()
            return carry

        @pl.when((s < LEVELS - 1) if side == DEC else (s > 0))
        def _():
            lax.fori_loop(0, PIECES, chained, 0)

        for j in range(3):
            z_copy(side, j).wait_send()
            az_copy(side, j).wait_send()
            f_copy(side, j).wait_send()
        for zz in range(4):
            x_copy(side, zz).wait_send()
            ac_copy(side, zz).wait_send()


def body(enc_weight, dec_weight, modulation, enc_inputs, dec_inputs, cotangent, timesteps):
    half = modulation.shape[2] // 2
    freqs = jnp.exp(-jnp.log(10000.0) * jnp.arange(half).astype(F32) / half)
    angles = timesteps.reshape(-1).astype(F32)[:, None] * freqs
    emb = jnp.concatenate([jnp.sin(angles), jnp.cos(angles)], axis=-1)
    dma = pltpu.SemaphoreType.DMA
    out, grams = pl.pallas_call(
        kernel,
        name="unet_backward",
        out_shape=(jax.ShapeDtypeStruct((ROWS, C), BF16), jax.ShapeDtypeStruct((2, OUT_ROWS, C), F32)),
        in_specs=[pl.BlockSpec(memory_space=pltpu.VMEM)] + [pl.BlockSpec(memory_space=pl.ANY)] * 6,
        out_specs=(pl.BlockSpec(memory_space=pltpu.VMEM), pl.BlockSpec(memory_space=pltpu.VMEM)),
        scratch_shapes=[
            pltpu.VMEM((2, C, C), BF16), pltpu.VMEM((2, C, C), BF16), pltpu.VMEM((2, 256, C), BF16),
            pltpu.VMEM((2, ROWS, C), BF16), pltpu.VMEM((2, ROWS, C), F32), pltpu.VMEM((2, ROWS, C), BF16),
            pltpu.VMEM((2, ROWS, C), BF16), pltpu.VMEM((2, ROWS, C), BF16), pltpu.VMEM((8, C), F32),
            pltpu.VMEM((2, 4 * ROWS, HALF), BF16), pltpu.VMEM((2, 4 * ROWS, HALF), BF16),
            pltpu.VMEM((2, HALF, HALF), BF16), pltpu.VMEM((2, HALF // 2, HALF), BF16),
            pltpu.VMEM((2, 3, BLOCK, HALF), BF16), pltpu.VMEM((2, HALF // 2, C), BF16), pltpu.VMEM((256, C), F32),
            pltpu.VMEM((2, OUT_ROWS, C), F32), pltpu.VMEM((2, 3, OUT_ROWS, C), BF16),
            pltpu.VMEM((2, 3, OUT_ROWS, C), BF16),
            dma((2, 4)), dma((2, PIECES, SPLIT)), dma((2, PIECES, SPLIT)), dma((2, 3)), dma((2, 3)),
            dma((2, 3, PIECES)), dma((2, 3, PIECES)), dma((2, 4)), dma((2, 4)), dma((2, 3)), dma((2, 3)),
            dma((2, 3)), dma((2, 3)), dma((2, 4)), dma((2, 4)), dma((2, 3)), dma((2, 3)),
        ],
        compiler_params=pltpu.CompilerParams(
            collective_id=0, has_side_effects=True, vmem_limit_bytes=40 * 1024 * 1024
        ),
    )(
        emb, *[pltpu.with_memory_space_constraint(a, pltpu.HBM) for a in (enc_weight.reshape(C, C), dec_weight.reshape(C, C), modulation.reshape(2, 256, C),
        enc_inputs.reshape(ROWS, C), dec_inputs.reshape(ROWS, C), cotangent.reshape(ROWS, C))],
    )
    return out.reshape(1, 2, 1, ROWS // 2, C), grams[None]


def solution(mesh):
    return jax.shard_map(
        body,
        mesh=mesh,
        in_specs=(
            P("section", None, None),
            P("section", None, None),
            P("section", None, None, None),
            P("section", None, ("dp", "rep"), None, None),
            P("section", None, ("dp", "rep"), None, None),
            P(None, ("dp", "rep"), None, None),
            P(None, ("dp", "rep"), None),
        ),
        out_specs=(
            P("section", None, ("dp", "rep"), None, None),
            P("section", None, ("dp", "rep"), None),
        ),
        check_vma=False,
    )
```

```python
import jax
import jax.numpy as jnp
from jax import lax
from jax.experimental import pallas as pl
from jax.experimental.pallas import tpu as pltpu
from jax.sharding import PartitionSpec as P

MESH = pl.DeviceIdType.MESH
F32 = jnp.float32
BF16 = jnp.bfloat16

C = 1280
HALF = C // 2
ROWS = 192
PIECE = 32
PIECES = ROWS // PIECE
SPLIT = 2
PART = C // SPLIT
FRAME = 24
LEVELS = 8
BLOCK = 80
OUT_ROWS = 40
PHASES = 6
REP_FIRST = 512
Z_FIRST = HALF - REP_FIRST
EARLY = (3, 3, 3, 1, 1, 0, 0, 0)
DENOM = 7864320.0
ENC, DEC = 0, 1


def kernel(
    emb_ref, enc_w, dec_w, mod_hbm, enc_u, dec_u, cot_hbm, out_ref, gram_ref,
    w, wt, mod, u, sg, chain_in, back, delta, gains,
    u4, d4, part, from_rep, from_z, from_z_both, from_rep_late, g, gram_acc, own_gram, send_gram, recv_gram,
    load_sem, chain_s, chain_r, u_s, u_r, d_s, d_r, x_s, x_r, z_s, z_r, zb_s, zb_r, xb_s, xb_r,
    az_s, az_r, ac_s, ac_r, f_s, f_r,
):
    s = lax.axis_index("section")
    dp = lax.axis_index("dp")
    r = lax.axis_index("rep")
    z, c = dp // 2, dp % 2
    zp, zg = z % 2, z // 2
    up = {"section": lax.rem(s + 1, LEVELS)}
    down = {"section": lax.rem(s + LEVELS - 1, LEVELS)}
    z_other = z + 1 - 2 * zp
    sibling = {"dp": z * 2 + 1 - c}
    pair_same = {"dp": z_other * 2 + c}
    pair_cross = {"dp": z_other * 2 + 1 - c}
    rep_other = {"rep": 1 - r}
    quad = [sibling, pair_same, pair_cross]
    quad_core = [1 - c, c, 1 - c]
    quad_zp = [zp, 1 - zp, 1 - zp]
    zg_of = [lax.rem(zg + 1 + j, 4) for j in range(3)]
    z_group = [{"dp": (zg_of[j] * 2 + zp) * 2 + c} for j in range(3)]
    gram_peer = [{"dp": z_other * 2 + c, "rep": 1 - r}, pair_same, rep_other]
    slot = zp * 2 + c
    quad_slot = [zp * 2 + 1 - c, (1 - zp) * 2 + c, (1 - zp) * 2 + 1 - c]

    def remote(src, dst, ss, rs, dev):
        return pltpu.make_async_remote_copy(
            src_ref=src, dst_ref=dst, send_sem=ss, recv_sem=rs, device_id=dev, device_id_type=MESH
        )

    def load(src, dst, a, b):
        return pltpu.make_async_copy(src, dst, load_sem.at[a, b])

    load(dec_u, u.at[DEC], DEC, 1).start()
    load(enc_u, u.at[ENC], ENC, 1).start()
    load(dec_w, w.at[DEC], DEC, 0).start()
    load(mod_hbm.at[DEC], mod.at[DEC], DEC, 2).start()
    cot_load = pltpu.make_async_copy(cot_hbm, chain_in.at[DEC], load_sem.at[0, 3])

    @pl.when(s == 0)
    def _():
        cot_load.start()

    load(enc_w, w.at[ENC], ENC, 0).start()
    load(mod_hbm.at[ENC], mod.at[ENC], ENC, 2).start()

    barrier = pltpu.get_barrier_semaphore()
    partners = [up, down, gram_peer[0], rep_other] + quad + z_group
    for dev in partners:
        pl.semaphore_signal(barrier, inc=1, device_id=dev, device_id_type=MESH)

    @pl.when(s == LEVELS - 1)
    def _():
        chain_in[ENC] = jnp.zeros((ROWS, C), BF16)

    def col(h):
        return pl.ds(pl.multiple_of(h * HALF, HALF), HALF)

    def rows(start, size, unit):
        return pl.ds(pl.multiple_of(start, unit), size)

    def prep(side):
        load(dec_w, w.at[side], side, 0).wait()
        load(mod_hbm.at[DEC], mod.at[side], side, 2).wait()
        sg[side] = jnp.dot(u[side], w[side], preferred_element_type=F32)
        e = emb_ref[...]
        hi = e.astype(BF16)
        rest = e - hi.astype(F32)
        mid = rest.astype(BF16)
        low = (rest - mid.astype(F32)).astype(BF16)
        table = mod[side]
        gains[...] = 1.0 + (
            jnp.dot(hi, table, preferred_element_type=F32)
            + (jnp.dot(mid, table, preferred_element_type=F32) + jnp.dot(low, table, preferred_element_type=F32))
        )

        def frame(f, carry):
            at = rows(f * FRAME, FRAME, 8)
            gain = gains[pl.ds(f, 1), :]
            pre = sg[side, at, :] * gain
            sigma = jax.nn.sigmoid(pre)
            sg[side, at, :] = sigma * (1.0 + pre * (1.0 - sigma)) * gain
            return carry

        lax.fori_loop(0, ROWS // FRAME, frame, 0)
        wt[side] = w[side].T

    def chain_copy(side, m, k):
        at = rows(m * PIECE, PIECE, PIECE)
        cols = pl.ds(k * PART, PART)
        dev = {"section": jnp.where(side == DEC, lax.rem(s + 1, LEVELS), lax.rem(s + LEVELS - 1, LEVELS))}
        return remote(
            back.at[side, at, cols], chain_in.at[side, at, cols], chain_s.at[side, m, k], chain_r.at[side, m, k], dev
        )

    def delta_copy(side, m, q):
        at = rows(m * PIECE, PIECE, PIECE)
        there = rows(slot * ROWS + m * PIECE, PIECE, PIECE)
        return remote(
            delta.at[side, at, col(quad_core[q])], d4.at[side, there], d_s.at[side, q, m], d_r.at[side, q, m], quad[q]
        )

    def u_copy(side, q):
        there = rows(slot * ROWS, ROWS, ROWS)
        return remote(u.at[side, :, col(quad_zp[q])], u4.at[side, there], u_s.at[side, q], u_r.at[side, q], quad[q])

    def level(side, m, incoming, sends):
        at = rows(m * PIECE, PIECE, PIECE)
        d = (incoming * sg[side, at, :]).astype(BF16)
        delta[side, at, :] = d
        for k in range(SPLIT):
            cols = pl.ds(k * PART, PART)
            back[side, at, cols] = jnp.dot(d, wt[side, :, cols], preferred_element_type=F32).astype(BF16)

            @pl.when(sends)
            def _():
                chain_copy(side, m, k).start()

    def share_delta(side, m):
        for q in range(3):
            delta_copy(side, m, q).start()
        at = rows(m * PIECE, PIECE, PIECE)
        d4[side, rows(slot * ROWS + m * PIECE, PIECE, PIECE), :] = delta[side, at, col(c)]

    def piece_rows(rr, zz):
        return rows((rr * 4 + zz) * BLOCK, BLOCK, 16)

    def x_copy(side, zz):
        return remote(
            part.at[side, piece_rows(1 - r, zz), pl.ds(0, REP_FIRST)], from_rep.at[side, rows(zz * BLOCK, BLOCK, 16)],
            x_s.at[side, zz], x_r.at[side, zz], rep_other,
        )

    def z_copy(side, j):
        return remote(
            part.at[side, piece_rows(r, zg_of[j]), pl.ds(0, REP_FIRST)], from_z.at[side, 2 - j],
            z_s.at[side, j], z_r.at[side, 2 - j], z_group[j],
        )

    def zb_copy(side, j, rr):
        return remote(
            part.at[side, piece_rows(rr, zg_of[j]), pl.ds(REP_FIRST, Z_FIRST)], from_z_both.at[side, 2 - j, rr],
            zb_s.at[side, j, rr], zb_r.at[side, 2 - j, rr], z_group[j],
        )

    def xb_copy(side):
        return remote(
            part.at[side, piece_rows(1 - r, zg), pl.ds(REP_FIRST, Z_FIRST)], from_rep_late.at[side],
            xb_s.at[side], xb_r.at[side], rep_other,
        )

    def z_first_sum(side, rr):
        total = part[side, piece_rows(rr, zg), pl.ds(REP_FIRST, Z_FIRST)].astype(F32)
        for j in range(3):
            total = total + from_z_both[side, j, rr].astype(F32)
        return total

    def g_piece(side, zz):
        return g.at[side, rows(zz * BLOCK, BLOCK, 16), col(c)]

    def az_copy(side, j):
        p = g_piece(side, zg)
        return remote(p, p, az_s.at[side, j], az_r.at[side, 2 - j], z_group[j])

    def ac_copy(side, zz):
        p = g_piece(side, zz)
        return remote(p, p, ac_s.at[side, zz], ac_r.at[side, zz], sibling)

    def f_copy(side, j):
        return remote(send_gram.at[side, j], recv_gram.at[side, j], f_s.at[side, j], f_r.at[side, j], gram_peer[j])

    def multiply_gathered(side, zz):
        base = 160 * zz + 80 * c
        start = jnp.minimum((base // 128) * 128, C - 256)
        cols = pl.ds(pl.multiple_of(start, 128), 256)
        gram_acc[...] = lax.dot_general(
            g[side, :, cols], g[side], (((0,), (0,)), ((), ())), preferred_element_type=F32
        )
        return base - start

    def phase(p, side):
        @pl.when(p == -1)
        def _():
            prep(side)

        @pl.when(p == 0)
        def _():
            for q in range(3):
                u_copy(side, q).wait_recv()

                def one(m, carry):
                    delta_copy(side, m, q).wait_recv()
                    return carry

                lax.fori_loop(0, PIECES, one, 0)
            part[side] = lax.dot_general(
                u4[side], d4[side], (((0,), (0,)), ((), ())), preferred_element_type=F32
            ).astype(BF16)
            for j in range(3):
                x_copy(side, zg_of[j]).start()
                zb_copy(side, j, 0).start()
                zb_copy(side, j, 1).start()
            x_copy(side, zg).start()

        @pl.when(p == 1)
        def _():
            for j in range(3):
                x_copy(side, zg_of[j]).wait_recv()
                at = piece_rows(r, zg_of[j])
                part[side, at, pl.ds(0, REP_FIRST)] = (
                    part[side, at, pl.ds(0, REP_FIRST)].astype(F32)
                    + from_rep[side, rows(zg_of[j] * BLOCK, BLOCK, 16), :].astype(F32)
                ).astype(BF16)
                z_copy(side, j).start()
            for j in range(3):
                zb_copy(side, 2 - j, 0).wait_recv()
                zb_copy(side, 2 - j, 1).wait_recv()
            part[side, piece_rows(1 - r, zg), pl.ds(REP_FIRST, Z_FIRST)] = z_first_sum(side, 1 - r).astype(BF16)
            xb_copy(side).start()

        @pl.when(p == 2)
        def _():
            x_copy(side, zg).wait_recv()
            total = part[side, piece_rows(r, zg), pl.ds(0, REP_FIRST)].astype(F32) + from_rep[
                side, rows(zg * BLOCK, BLOCK, 16), :
            ].astype(F32)
            for j in range(3):
                z_copy(side, 2 - j).wait_recv()
                total = total + from_z[side, j].astype(F32)
            xb_copy(side).wait_recv()
            late_total = z_first_sum(side, r) + from_rep_late[side].astype(F32)
            at = rows(zg * BLOCK, BLOCK, 16)
            g[side, at, pl.ds(pl.multiple_of(c * HALF, 128), REP_FIRST)] = total.astype(BF16)
            g[side, at, pl.ds(pl.multiple_of(c * HALF + REP_FIRST, 128), Z_FIRST)] = late_total.astype(BF16)
            for j in range(3):
                az_copy(side, j).start()
            ac_copy(side, zg).start()

        @pl.when(p == 3)
        def _():
            for j in range(3):
                az_copy(side, 2 - j).wait_recv()
                ac_copy(side, zg_of[j]).start()

        @pl.when(p == 4)
        def _():
            for zz in range(4):
                ac_copy(side, zz).wait_recv()

            def there(k, carry):
                offset = multiply_gathered(side, jnp.where(k == 0, z_other, z))

                @pl.when(k == 0)
                def _():
                    for j, rr in ((0, 1 - r), (1, r)):
                        send_gram[side, j] = gram_acc[rows(offset + 40 * rr, OUT_ROWS, 8), :].astype(BF16)
                        f_copy(side, j).start()

                @pl.when(k == 1)
                def _():
                    send_gram[side, 2] = gram_acc[rows(offset + 40 * (1 - r), OUT_ROWS, 8), :].astype(BF16)
                    f_copy(side, 2).start()
                    own_gram[side] = gram_acc[rows(offset + 40 * r, OUT_ROWS, 8), :]

                return carry

            lax.fori_loop(0, 2, there, 0)

        @pl.when(p == 5)
        def _():
            gram = own_gram[side]
            for j in range(3):
                f_copy(side, j).wait_recv()
                gram = gram + recv_gram[side, j].astype(F32)
            gram_ref[side] = gram / DENOM

    early = jnp.int32(0)
    for level_index, count in enumerate(EARLY):
        early = jnp.where(s == level_index, count, early)

    def step(i, carry):
        last = s == LEVELS - 1
        is_chain = i < 2 * PIECES
        is_dec = is_chain & jnp.where(last, i % 2 == 0, i < PIECES)
        is_enc = is_chain & jnp.where(last, i % 2 == 1, i >= PIECES)
        m = jnp.where(last, lax.div(i, 2), lax.rem(i, PIECES))

        @pl.when(is_dec)
        def _():
            @pl.when(s > 0)
            def _():
                for k in range(SPLIT):
                    chain_copy(DEC, m, k).wait_recv()

            @pl.when((s == 0) & (m == 0))
            def _():
                cot_load.wait()

            at = rows(m * PIECE, PIECE, PIECE)
            level(DEC, m, chain_in[DEC, at, :].astype(F32), s < LEVELS - 1)
            share_delta(DEC, m)

        @pl.when(is_enc)
        def _():
            @pl.when(s < LEVELS - 1)
            def _():
                for k in range(SPLIT):
                    chain_copy(ENC, m, k).wait_recv()

            at = rows(m * PIECE, PIECE, PIECE)
            both = (back[DEC, at, :].astype(F32) + chain_in[ENC, at, :].astype(F32)).astype(BF16)
            level(ENC, m, both.astype(F32), s > 0)
            share_delta(ENC, m)
            out_ref[at, :] = back[ENC, at, :]

        middle = i == PIECES - 1
        late = i >= 2 * PIECES
        lead = jnp.where(s == 0, 1, 0)
        n = jnp.where(middle, lead + early, jnp.where(late, 2, 0))

        def event(j, carry):
            p = jnp.where(middle, j - lead, i - 2 * PIECES)
            side = jnp.where(middle, jnp.where(p < 0, ENC, DEC), 1 - j)
            done = late & (side == DEC) & (p < early)

            @pl.when(jnp.logical_not(done))
            def _():
                phase(p, side)

            return carry

        lax.fori_loop(0, n, event, 0)

        return carry

    load(dec_u, u.at[DEC], DEC, 1).wait()
    load(enc_u, u.at[ENC], ENC, 1).wait()

    def prepare(j, carry):
        prep(1 - j)
        return carry

    lax.fori_loop(0, jnp.where(s == 0, 1, 2), prepare, 0)
    pl.semaphore_wait(barrier, len(partners))
    for side in (DEC, ENC):
        for q in range(3):
            u_copy(side, q).start()
        u4[side, rows(slot * ROWS, ROWS, ROWS), :] = u[side, :, col(zp)]
    lax.fori_loop(0, 2 * PIECES + PHASES, step, 0)

    for side in (DEC, ENC):
        for q in range(3):
            u_copy(side, q).wait_send()

            def sent(m, carry):
                delta_copy(side, m, q).wait_send()
                return carry

            lax.fori_loop(0, PIECES, sent, 0)

        def chained(m, carry):
            for k in range(SPLIT):
                chain_copy(side, m, k).wait_send()
            return carry

        @pl.when((s < LEVELS - 1) if side == DEC else (s > 0))
        def _():
            lax.fori_loop(0, PIECES, chained, 0)

        for j in range(3):
            z_copy(side, j).wait_send()
            zb_copy(side, j, 0).wait_send()
            zb_copy(side, j, 1).wait_send()
            az_copy(side, j).wait_send()
            f_copy(side, j).wait_send()
        xb_copy(side).wait_send()
        for zz in range(4):
            x_copy(side, zz).wait_send()
            ac_copy(side, zz).wait_send()


def body(enc_weight, dec_weight, modulation, enc_inputs, dec_inputs, cotangent, timesteps):
    half = modulation.shape[2] // 2
    freqs = jnp.exp(-jnp.log(10000.0) * jnp.arange(half).astype(F32) / half)
    angles = timesteps.reshape(-1).astype(F32)[:, None] * freqs
    emb = jnp.concatenate([jnp.sin(angles), jnp.cos(angles)], axis=-1)
    dma = pltpu.SemaphoreType.DMA
    out, grams = pl.pallas_call(
        kernel,
        name="unet_backward",
        out_shape=(jax.ShapeDtypeStruct((ROWS, C), BF16), jax.ShapeDtypeStruct((2, OUT_ROWS, C), F32)),
        in_specs=[pl.BlockSpec(memory_space=pltpu.VMEM)] + [pl.BlockSpec(memory_space=pl.ANY)] * 6,
        out_specs=(pl.BlockSpec(memory_space=pltpu.VMEM), pl.BlockSpec(memory_space=pltpu.VMEM)),
        scratch_shapes=[
            pltpu.VMEM((2, C, C), BF16), pltpu.VMEM((2, C, C), BF16), pltpu.VMEM((2, 256, C), BF16),
            pltpu.VMEM((2, ROWS, C), BF16), pltpu.VMEM((2, ROWS, C), F32), pltpu.VMEM((2, ROWS, C), BF16),
            pltpu.VMEM((2, ROWS, C), BF16), pltpu.VMEM((2, ROWS, C), BF16), pltpu.VMEM((8, C), F32),
            pltpu.VMEM((2, 4 * ROWS, HALF), BF16), pltpu.VMEM((2, 4 * ROWS, HALF), BF16),
            pltpu.VMEM((2, HALF, HALF), BF16), pltpu.VMEM((2, HALF // 2, REP_FIRST), BF16),
            pltpu.VMEM((2, 3, BLOCK, REP_FIRST), BF16),
            pltpu.VMEM((2, 3, 2, BLOCK, Z_FIRST), BF16), pltpu.VMEM((2, BLOCK, Z_FIRST), BF16), pltpu.VMEM((2, HALF // 2, C), BF16), pltpu.VMEM((256, C), F32),
            pltpu.VMEM((2, OUT_ROWS, C), F32), pltpu.VMEM((2, 3, OUT_ROWS, C), BF16),
            pltpu.VMEM((2, 3, OUT_ROWS, C), BF16),
            dma((2, 4)), dma((2, PIECES, SPLIT)), dma((2, PIECES, SPLIT)), dma((2, 3)), dma((2, 3)),
            dma((2, 3, PIECES)), dma((2, 3, PIECES)), dma((2, 4)), dma((2, 4)), dma((2, 3)), dma((2, 3)),
            dma((2, 3, 2)), dma((2, 3, 2)), dma((2,)), dma((2,)),
            dma((2, 3)), dma((2, 3)), dma((2, 4)), dma((2, 4)), dma((2, 3)), dma((2, 3)),
        ],
        compiler_params=pltpu.CompilerParams(
            collective_id=0, has_side_effects=True, vmem_limit_bytes=40 * 1024 * 1024
        ),
    )(
        emb, *[pltpu.with_memory_space_constraint(a, pltpu.HBM) for a in (enc_weight.reshape(C, C), dec_weight.reshape(C, C), modulation.reshape(2, 256, C),
        enc_inputs.reshape(ROWS, C), dec_inputs.reshape(ROWS, C), cotangent.reshape(ROWS, C))],
    )
    return out.reshape(1, 2, 1, ROWS // 2, C), grams[None]


def solution(mesh):
    return jax.shard_map(
        body,
        mesh=mesh,
        in_specs=(
            P("section", None, None),
            P("section", None, None),
            P("section", None, None, None),
            P("section", None, ("dp", "rep"), None, None),
            P("section", None, ("dp", "rep"), None, None),
            P(None, ("dp", "rep"), None, None),
            P(None, ("dp", "rep"), None),
        ),
        out_specs=(
            P("section", None, ("dp", "rep"), None, None),
            P("section", None, ("dp", "rep"), None),
        ),
        check_vma=False,
    )
```

```python
import jax
import jax.numpy as jnp
from jax import lax
from jax.experimental import pallas as pl
from jax.experimental.pallas import tpu as pltpu
from jax.sharding import PartitionSpec as P

MESH = pl.DeviceIdType.MESH
F32 = jnp.float32
BF16 = jnp.bfloat16

C = 1280
HALF = C // 2
ROWS = 192
PIECE = 32
PIECES = ROWS // PIECE
SPLIT = 2
PART = C // SPLIT
FRAME = 24
LEVELS = 8
BLOCK = 80
OUT_ROWS = 40
PHASES = 6
REP_FIRST = 512
Z_FIRST = HALF - REP_FIRST
EARLY = (3, 3, 3, 1, 1, 0, 0, 0)
DENOM = 7864320.0
ENC, DEC = 0, 1


def kernel(
    emb_ref, enc_w, dec_w, mod_hbm, enc_u, dec_u, cot_hbm, out_ref, gram_ref,
    w, wt, mod, u, sg, chain_in, back, delta, gains,
    u4, d4, part, from_rep, from_z, from_z_both, from_rep_late, g, gram_acc, own_gram, send_gram, recv_gram,
    load_sem, chain_s, chain_r, u_s, u_r, d_s, d_r, x_s, x_r, z_s, z_r, zb_s, zb_r, xb_s, xb_r,
    az_s, az_r, ac_s, ac_r, f_s, f_r,
):
    s = lax.axis_index("section")
    dp = lax.axis_index("dp")
    r = lax.axis_index("rep")
    z, c = dp // 2, dp % 2
    zp, zg = z % 2, z // 2
    up = {"section": lax.rem(s + 1, LEVELS)}
    down = {"section": lax.rem(s + LEVELS - 1, LEVELS)}
    z_other = z + 1 - 2 * zp
    sibling = {"dp": z * 2 + 1 - c}
    pair_same = {"dp": z_other * 2 + c}
    pair_cross = {"dp": z_other * 2 + 1 - c}
    rep_other = {"rep": 1 - r}
    quad = [sibling, pair_same, pair_cross]
    quad_core = [1 - c, c, 1 - c]
    quad_zp = [zp, 1 - zp, 1 - zp]
    zg_of = [lax.rem(zg + 1 + j, 4) for j in range(3)]
    z_group = [{"dp": (zg_of[j] * 2 + zp) * 2 + c} for j in range(3)]
    gram_peer = [{"dp": z_other * 2 + c, "rep": 1 - r}, pair_same, rep_other]
    slot = zp * 2 + c
    quad_slot = [zp * 2 + 1 - c, (1 - zp) * 2 + c, (1 - zp) * 2 + 1 - c]

    def remote(src, dst, ss, rs, dev):
        return pltpu.make_async_remote_copy(
            src_ref=src, dst_ref=dst, send_sem=ss, recv_sem=rs, device_id=dev, device_id_type=MESH
        )

    def load(src, dst, a, b):
        return pltpu.make_async_copy(src, dst, load_sem.at[a, b])

    load(dec_u, u.at[DEC], DEC, 1).start()
    load(enc_u, u.at[ENC], ENC, 1).start()
    load(dec_w, w.at[DEC], DEC, 0).start()
    load(mod_hbm.at[DEC], mod.at[DEC], DEC, 2).start()
    cot_load = pltpu.make_async_copy(cot_hbm, chain_in.at[DEC], load_sem.at[0, 3])

    @pl.when(s == 0)
    def _():
        cot_load.start()

    load(enc_w, w.at[ENC], ENC, 0).start()
    load(mod_hbm.at[ENC], mod.at[ENC], ENC, 2).start()

    barrier = pltpu.get_barrier_semaphore()
    partners = [up, down, gram_peer[0], rep_other] + quad + z_group
    for dev in partners:
        pl.semaphore_signal(barrier, inc=1, device_id=dev, device_id_type=MESH)

    @pl.when(s == LEVELS - 1)
    def _():
        chain_in[ENC] = jnp.zeros((ROWS, C), BF16)

    def col(h):
        return pl.ds(pl.multiple_of(h * HALF, HALF), HALF)

    def rows(start, size, unit):
        return pl.ds(pl.multiple_of(start, unit), size)

    def prep(side):
        load(dec_w, w.at[side], side, 0).wait()
        load(mod_hbm.at[DEC], mod.at[side], side, 2).wait()
        sg[side] = jnp.dot(u[side], w[side], preferred_element_type=F32)
        e = emb_ref[...]
        hi = e.astype(BF16)
        rest = e - hi.astype(F32)
        mid = rest.astype(BF16)
        low = (rest - mid.astype(F32)).astype(BF16)
        table = mod[side]
        gains[...] = 1.0 + (
            jnp.dot(hi, table, preferred_element_type=F32)
            + (jnp.dot(mid, table, preferred_element_type=F32) + jnp.dot(low, table, preferred_element_type=F32))
        )

        def frame(f, carry):
            at = rows(f * FRAME, FRAME, 8)
            gain = gains[pl.ds(f, 1), :]
            pre = sg[side, at, :] * gain
            sigma = jax.nn.sigmoid(pre)
            sg[side, at, :] = sigma * (1.0 + pre * (1.0 - sigma)) * gain
            return carry

        lax.fori_loop(0, ROWS // FRAME, frame, 0)
        wt[side] = w[side].T

    def chain_copy(side, m, k):
        at = rows(m * PIECE, PIECE, PIECE)
        cols = pl.ds(k * PART, PART)
        dev = {"section": jnp.where(side == DEC, lax.rem(s + 1, LEVELS), lax.rem(s + LEVELS - 1, LEVELS))}
        return remote(
            back.at[side, at, cols], chain_in.at[side, at, cols], chain_s.at[side, m, k], chain_r.at[side, m, k], dev
        )

    def delta_copy(side, m, q):
        at = rows(m * PIECE, PIECE, PIECE)
        there = rows(slot * ROWS + m * PIECE, PIECE, PIECE)
        return remote(
            delta.at[side, at, col(quad_core[q])], d4.at[side, there], d_s.at[side, q, m], d_r.at[side, q, m], quad[q]
        )

    def u_copy(side, q):
        there = rows(slot * ROWS, ROWS, ROWS)
        return remote(u.at[side, :, col(quad_zp[q])], u4.at[side, there], u_s.at[side, q], u_r.at[side, q], quad[q])

    def level(side, m, incoming, sends):
        at = rows(m * PIECE, PIECE, PIECE)
        d = (incoming * sg[side, at, :]).astype(BF16)
        delta[side, at, :] = d
        for k in range(SPLIT):
            cols = pl.ds(k * PART, PART)
            back[side, at, cols] = jnp.dot(d, wt[side, :, cols], preferred_element_type=F32).astype(BF16)

            @pl.when(sends)
            def _():
                chain_copy(side, m, k).start()

    def share_delta(side, m):
        for q in range(3):
            delta_copy(side, m, q).start()
        at = rows(m * PIECE, PIECE, PIECE)
        d4[side, rows(slot * ROWS + m * PIECE, PIECE, PIECE), :] = delta[side, at, col(c)]

    def piece_rows(rr, zz):
        return rows((rr * 4 + zz) * BLOCK, BLOCK, 16)

    def x_copy(side, zz):
        return remote(
            part.at[side, piece_rows(1 - r, zz), pl.ds(0, REP_FIRST)], from_rep.at[side, rows(zz * BLOCK, BLOCK, 16)],
            x_s.at[side, zz], x_r.at[side, zz], rep_other,
        )

    def z_copy(side, j):
        return remote(
            part.at[side, piece_rows(r, zg_of[j]), pl.ds(0, REP_FIRST)], from_z.at[side, 2 - j],
            z_s.at[side, j], z_r.at[side, 2 - j], z_group[j],
        )

    def zb_copy(side, j, rr):
        return remote(
            part.at[side, piece_rows(rr, zg_of[j]), pl.ds(REP_FIRST, Z_FIRST)], from_z_both.at[side, 2 - j, rr],
            zb_s.at[side, j, rr], zb_r.at[side, 2 - j, rr], z_group[j],
        )

    def xb_copy(side):
        return remote(
            part.at[side, piece_rows(1 - r, zg), pl.ds(REP_FIRST, Z_FIRST)], from_rep_late.at[side],
            xb_s.at[side], xb_r.at[side], rep_other,
        )

    def z_first_sum(side, rr):
        total = part[side, piece_rows(rr, zg), pl.ds(REP_FIRST, Z_FIRST)].astype(F32)
        for j in range(3):
            total = total + from_z_both[side, j, rr].astype(F32)
        return total

    def g_piece(side, zz):
        return g.at[side, rows(zz * BLOCK, BLOCK, 16), col(c)]

    def az_copy(side, j):
        p = g_piece(side, zg)
        return remote(p, p, az_s.at[side, j], az_r.at[side, 2 - j], z_group[j])

    def ac_copy(side, zz):
        p = g_piece(side, zz)
        return remote(p, p, ac_s.at[side, zz], ac_r.at[side, zz], sibling)

    def f_copy(side, j):
        return remote(send_gram.at[side, j], recv_gram.at[side, j], f_s.at[side, j], f_r.at[side, j], gram_peer[j])

    def multiply_gathered(side, zz):
        base = 160 * zz + 80 * c
        start = jnp.minimum((base // 128) * 128, C - 256)
        cols = pl.ds(pl.multiple_of(start, 128), 256)
        gram_acc[...] = lax.dot_general(
            g[side, :, cols], g[side], (((0,), (0,)), ((), ())), preferred_element_type=F32
        )
        return base - start

    def phase(p, side):
        @pl.when(p == -1)
        def _():
            prep(side)

        @pl.when(p == 0)
        def _():
            for q in range(3):
                u_copy(side, q).wait_recv()

                def one(m, carry):
                    delta_copy(side, m, q).wait_recv()
                    return carry

                lax.fori_loop(0, PIECES, one, 0)
            for cols, copies in (
                (pl.ds(0, REP_FIRST), [x_copy(side, zz) for zz in zg_of + [zg]]),
                (pl.ds(REP_FIRST, Z_FIRST), [zb_copy(side, j, rr) for j in range(3) for rr in range(2)]),
            ):
                part[side, :, cols] = lax.dot_general(
                    u4[side], d4[side, :, cols], (((0,), (0,)), ((), ())), preferred_element_type=F32
                ).astype(BF16)
                for copy in copies:
                    copy.start()

        @pl.when(p == 1)
        def _():
            for j in range(3):
                x_copy(side, zg_of[j]).wait_recv()
                at = piece_rows(r, zg_of[j])
                part[side, at, pl.ds(0, REP_FIRST)] = (
                    part[side, at, pl.ds(0, REP_FIRST)].astype(F32)
                    + from_rep[side, rows(zg_of[j] * BLOCK, BLOCK, 16), :].astype(F32)
                ).astype(BF16)
                z_copy(side, j).start()
            for j in range(3):
                zb_copy(side, 2 - j, 0).wait_recv()
                zb_copy(side, 2 - j, 1).wait_recv()
            part[side, piece_rows(1 - r, zg), pl.ds(REP_FIRST, Z_FIRST)] = z_first_sum(side, 1 - r).astype(BF16)
            xb_copy(side).start()

        @pl.when(p == 2)
        def _():
            x_copy(side, zg).wait_recv()
            total = part[side, piece_rows(r, zg), pl.ds(0, REP_FIRST)].astype(F32) + from_rep[
                side, rows(zg * BLOCK, BLOCK, 16), :
            ].astype(F32)
            for j in range(3):
                z_copy(side, 2 - j).wait_recv()
                total = total + from_z[side, j].astype(F32)
            xb_copy(side).wait_recv()
            late_total = z_first_sum(side, r) + from_rep_late[side].astype(F32)
            at = rows(zg * BLOCK, BLOCK, 16)
            g[side, at, pl.ds(pl.multiple_of(c * HALF, 128), REP_FIRST)] = total.astype(BF16)
            g[side, at, pl.ds(pl.multiple_of(c * HALF + REP_FIRST, 128), Z_FIRST)] = late_total.astype(BF16)
            for j in (1, 0, 2):
                az_copy(side, j).start()
            ac_copy(side, zg).start()

        @pl.when(p == 3)
        def _():
            for j in (0, 2, 1):
                az_copy(side, 2 - j).wait_recv()
                ac_copy(side, zg_of[j]).start()

        @pl.when(p == 4)
        def _():
            for zz in range(4):
                ac_copy(side, zz).wait_recv()

            def there(k, carry):
                offset = multiply_gathered(side, jnp.where(k == 0, z_other, z))

                @pl.when(k == 0)
                def _():
                    for j, rr in ((0, 1 - r), (1, r)):
                        send_gram[side, j] = gram_acc[rows(offset + 40 * rr, OUT_ROWS, 8), :].astype(BF16)
                        f_copy(side, j).start()

                @pl.when(k == 1)
                def _():
                    send_gram[side, 2] = gram_acc[rows(offset + 40 * (1 - r), OUT_ROWS, 8), :].astype(BF16)
                    f_copy(side, 2).start()
                    own_gram[side] = gram_acc[rows(offset + 40 * r, OUT_ROWS, 8), :]

                return carry

            lax.fori_loop(0, 2, there, 0)

        @pl.when(p == 5)
        def _():
            gram = own_gram[side]
            for j in range(3):
                f_copy(side, j).wait_recv()
                gram = gram + recv_gram[side, j].astype(F32)
            gram_ref[side] = gram / DENOM

    early = jnp.int32(0)
    for level_index, count in enumerate(EARLY):
        early = jnp.where(s == level_index, count, early)

    def step(i, carry):
        last = s == LEVELS - 1
        is_chain = i < 2 * PIECES
        is_dec = is_chain & jnp.where(last, i % 2 == 0, i < PIECES)
        is_enc = is_chain & jnp.where(last, i % 2 == 1, i >= PIECES)
        m = jnp.where(last, lax.div(i, 2), lax.rem(i, PIECES))

        @pl.when(is_dec)
        def _():
            @pl.when(s > 0)
            def _():
                for k in range(SPLIT):
                    chain_copy(DEC, m, k).wait_recv()

            @pl.when((s == 0) & (m == 0))
            def _():
                cot_load.wait()

            at = rows(m * PIECE, PIECE, PIECE)
            level(DEC, m, chain_in[DEC, at, :].astype(F32), s < LEVELS - 1)
            share_delta(DEC, m)

        @pl.when(is_enc)
        def _():
            @pl.when(s < LEVELS - 1)
            def _():
                for k in range(SPLIT):
                    chain_copy(ENC, m, k).wait_recv()

            at = rows(m * PIECE, PIECE, PIECE)
            both = (back[DEC, at, :].astype(F32) + chain_in[ENC, at, :].astype(F32)).astype(BF16)
            level(ENC, m, both.astype(F32), s > 0)
            share_delta(ENC, m)
            out_ref[at, :] = back[ENC, at, :]

        middle = i == PIECES - 1
        late = i >= 2 * PIECES
        lead = jnp.where(s == 0, 1, 0)
        n = jnp.where(middle, lead + early, jnp.where(late, 2, 0))

        def event(j, carry):
            p = jnp.where(middle, j - lead, i - 2 * PIECES)
            side = jnp.where(middle, jnp.where(p < 0, ENC, DEC), 1 - j)
            done = late & (side == DEC) & (p < early)

            @pl.when(jnp.logical_not(done))
            def _():
                phase(p, side)

            return carry

        lax.fori_loop(0, n, event, 0)

        return carry

    load(dec_u, u.at[DEC], DEC, 1).wait()
    load(enc_u, u.at[ENC], ENC, 1).wait()

    def prepare(j, carry):
        prep(1 - j)
        return carry

    lax.fori_loop(0, jnp.where(s == 0, 1, 2), prepare, 0)
    pl.semaphore_wait(barrier, len(partners))
    for side in (DEC, ENC):
        for q in range(3):
            u_copy(side, q).start()
        u4[side, rows(slot * ROWS, ROWS, ROWS), :] = u[side, :, col(zp)]
    lax.fori_loop(0, 2 * PIECES + PHASES, step, 0)

    for side in (DEC, ENC):
        for q in range(3):
            u_copy(side, q).wait_send()

            def sent(m, carry):
                delta_copy(side, m, q).wait_send()
                return carry

            lax.fori_loop(0, PIECES, sent, 0)

        def chained(m, carry):
            for k in range(SPLIT):
                chain_copy(side, m, k).wait_send()
            return carry

        @pl.when((s < LEVELS - 1) if side == DEC else (s > 0))
        def _():
            lax.fori_loop(0, PIECES, chained, 0)

        for j in range(3):
            z_copy(side, j).wait_send()
            zb_copy(side, j, 0).wait_send()
            zb_copy(side, j, 1).wait_send()
            az_copy(side, j).wait_send()
            f_copy(side, j).wait_send()
        xb_copy(side).wait_send()
        for zz in range(4):
            x_copy(side, zz).wait_send()
            ac_copy(side, zz).wait_send()


def body(enc_weight, dec_weight, modulation, enc_inputs, dec_inputs, cotangent, timesteps):
    half = modulation.shape[2] // 2
    freqs = jnp.exp(-jnp.log(10000.0) * jnp.arange(half).astype(F32) / half)
    angles = timesteps.reshape(-1).astype(F32)[:, None] * freqs
    emb = jnp.concatenate([jnp.sin(angles), jnp.cos(angles)], axis=-1)
    dma = pltpu.SemaphoreType.DMA
    out, grams = pl.pallas_call(
        kernel,
        name="unet_backward",
        out_shape=(jax.ShapeDtypeStruct((ROWS, C), BF16), jax.ShapeDtypeStruct((2, OUT_ROWS, C), F32)),
        in_specs=[pl.BlockSpec(memory_space=pltpu.VMEM)] + [pl.BlockSpec(memory_space=pl.ANY)] * 6,
        out_specs=(pl.BlockSpec(memory_space=pltpu.VMEM), pl.BlockSpec(memory_space=pltpu.VMEM)),
        scratch_shapes=[
            pltpu.VMEM((2, C, C), BF16), pltpu.VMEM((2, C, C), BF16), pltpu.VMEM((2, 256, C), BF16),
            pltpu.VMEM((2, ROWS, C), BF16), pltpu.VMEM((2, ROWS, C), F32), pltpu.VMEM((2, ROWS, C), BF16),
            pltpu.VMEM((2, ROWS, C), BF16), pltpu.VMEM((2, ROWS, C), BF16), pltpu.VMEM((8, C), F32),
            pltpu.VMEM((2, 4 * ROWS, HALF), BF16), pltpu.VMEM((2, 4 * ROWS, HALF), BF16),
            pltpu.VMEM((2, HALF, HALF), BF16), pltpu.VMEM((2, HALF // 2, REP_FIRST), BF16),
            pltpu.VMEM((2, 3, BLOCK, REP_FIRST), BF16),
            pltpu.VMEM((2, 3, 2, BLOCK, Z_FIRST), BF16), pltpu.VMEM((2, BLOCK, Z_FIRST), BF16), pltpu.VMEM((2, HALF // 2, C), BF16), pltpu.VMEM((256, C), F32),
            pltpu.VMEM((2, OUT_ROWS, C), F32), pltpu.VMEM((2, 3, OUT_ROWS, C), BF16),
            pltpu.VMEM((2, 3, OUT_ROWS, C), BF16),
            dma((2, 4)), dma((2, PIECES, SPLIT)), dma((2, PIECES, SPLIT)), dma((2, 3)), dma((2, 3)),
            dma((2, 3, PIECES)), dma((2, 3, PIECES)), dma((2, 4)), dma((2, 4)), dma((2, 3)), dma((2, 3)),
            dma((2, 3, 2)), dma((2, 3, 2)), dma((2,)), dma((2,)),
            dma((2, 3)), dma((2, 3)), dma((2, 4)), dma((2, 4)), dma((2, 3)), dma((2, 3)),
        ],
        compiler_params=pltpu.CompilerParams(
            collective_id=0, has_side_effects=True, vmem_limit_bytes=40 * 1024 * 1024
        ),
    )(
        emb, *[pltpu.with_memory_space_constraint(a, pltpu.HBM) for a in (enc_weight.reshape(C, C), dec_weight.reshape(C, C), modulation.reshape(2, 256, C),
        enc_inputs.reshape(ROWS, C), dec_inputs.reshape(ROWS, C), cotangent.reshape(ROWS, C))],
    )
    return out.reshape(1, 2, 1, ROWS // 2, C), grams[None]


def solution(mesh):
    return jax.shard_map(
        body,
        mesh=mesh,
        in_specs=(
            P("section", None, None),
            P("section", None, None),
            P("section", None, None, None),
            P("section", None, ("dp", "rep"), None, None),
            P("section", None, ("dp", "rep"), None, None),
            P(None, ("dp", "rep"), None, None),
            P(None, ("dp", "rep"), None),
        ),
        out_specs=(
            P("section", None, ("dp", "rep"), None, None),
            P("section", None, ("dp", "rep"), None),
        ),
        check_vma=False,
    )
```
